512 devices in a mesh: gx: 16 (over z, core), gy: 32 (over x, y).
Axes of the slice: x: 4, y: 8, z: 8, core: 2. Of those that a mesh axis runs over, the one named last changes fastest.
Arguments:
- state: float32 [65536, 6, 512], P(('gx', 'gy')), may hold values from -6 to 6
- levels: int32 [65536], P(('gx', 'gy')), may hold values from 0 to 2
- face_source: int32 [393216], P(('gx', 'gy')), may hold values from -1 to 895, as said below
- face_send: int32 [512, 4, 32], P(('gx', 'gy')), may hold values from 0 to 767, as said below
- mort_owner: int32 [512, 32, 1], P(('gx', 'gy')), may hold values from -1 to 767, as said below
- mort_child: int32 [512, 32, 4], P(('gx', 'gy')), may hold values from -1 to 767, as said below
- flux_jac: float32 [3, 6, 6], replicated, may hold values from -1.75 to 1.75
- penalty: float32 [6], replicated, may hold values from 0.5 to 1.5
Outputs:
- increment: float32 [65536, 6, 512], P(('gx', 'gy'))
The draws below stay inside these ranges and needn't reach their ends.
Inputs may be any that keep to these rules, and one draw needn't show every extreme that they name: `face_source`: values 0 to 767 name a face of the same device (a face naming itself has no jump); 768 + o * 32 + c names slot c of arrived block o; -1 marks a face on a mortar. Faces paired across devices see each other. `face_send`: local face slots, all distinct on one device, none on a mortar. `mort_owner`: entry [y', k] of device (x, y) is its large face whose four children lie on device (x, y') at slots 4 k to 4 k + 3 of that device's mort_child row y, quadrant = slot modulo 4; -1 where unused. Every device owns one mortar whose children lie on the next device along gy, wrapping; any other pair of devices with the same gx index, a device with itself included, may share a mortar or not, and owners differ in how many they hold. `mort_child`: entry [y, j] of a device is its face on quadrant j modulo 4 of mortar j // 4 owned by device y of the same gx index; -1 where unused, in whole groups of four.
All inputs are finite; a program needn't handle non-finite values.
Results may differ from the reference program's by a relative error of at most 0.0003.
Values sent between devices are 32-bit elements; how exact they have to be, the bound alone decides.
No kernel may reach another device: no remote copies, remote signals or barrier semaphores. Data moves between devices by JAX's collectives and lax.ppermute only.
A program may use at most 64 MiB of HBM per device.

```python
import jax
import jax.numpy as jnp
import numpy as np
from jax import lax

P_SIZE = 7
FIELDS = 6
NODES = 512
FNODES = 64
TRACE = 384
E_DEV = 128
CAP = 32
MORT_PAIR = 1
MCAP = 4
ELEMS = 65536
N_GX = 16
N_GY = 32


def build_lists(key):
    slots = 6 * E_DEV
    devices_all = N_GX * N_GY
    perm_keys = jax.random.split(jax.random.fold_in(key, 101), devices_all)
    orders = jax.vmap(lambda single: jax.random.permutation(single, slots))(perm_keys).astype(jnp.int32)
    heat = jax.random.randint(jax.random.fold_in(key, 102), (N_GX, N_GY, 1), 1, 5)
    coin = jax.random.randint(jax.random.fold_in(key, 103), (N_GX, N_GY, N_GY), 0, 4)
    counts = jnp.where(coin < heat, MORT_PAIR, 0).astype(jnp.int32)
    column = jnp.arange(N_GY)
    forced = column[None, :] == (column[:, None] + 1) % N_GY
    counts = jnp.where(forced[None, :, :], MORT_PAIR, counts).astype(jnp.int32)
    owner_count = counts.reshape(devices_all, N_GY)
    child_count = counts.transpose(0, 2, 1).reshape(devices_all, N_GY)
    base_owner = 4 * CAP
    base_child = base_owner + N_GY * MORT_PAIR
    base_local = base_child + N_GY * MCAP
    pair_pos = jnp.arange(MORT_PAIR)
    owner_live = pair_pos[None, None, :] < owner_count[:, :, None]
    owner_faces = orders[:, base_owner:base_child].reshape(devices_all, N_GY, MORT_PAIR)
    mort_owner = jnp.where(owner_live, owner_faces, -1).astype(jnp.int32)
    slot_pos = jnp.arange(MCAP)
    child_live = (slot_pos // 4)[None, None, :] < child_count[:, :, None]
    child_faces = orders[:, base_child:base_local].reshape(devices_all, N_GY, MCAP)
    mort_child = jnp.where(child_live, child_faces, -1).astype(jnp.int32)
    face_send = orders[:, :4 * CAP].reshape(devices_all, 4, CAP)
    position = jnp.arange(slots)
    conf_src = slots + (3 - position // CAP) * CAP + position % CAP
    relative = position - base_local
    partner = jnp.clip(base_local + relative + 1 - 2 * (relative % 2), 0, slots - 1)
    local_src = jnp.take_along_axis(orders, jnp.broadcast_to(partner, (devices_all, slots)), axis=1)
    mortar_src = jnp.concatenate([jnp.where(owner_live, -1, owner_faces).reshape(devices_all, -1), jnp.where(child_live, -1, child_faces).reshape(devices_all, -1)], axis=1)
    by_position = jnp.concatenate([jnp.broadcast_to(conf_src[:4 * CAP], (devices_all, 4 * CAP)), mortar_src, local_src[:, base_local:]], axis=1).astype(jnp.int32)
    rows = jnp.broadcast_to(jnp.arange(devices_all)[:, None], (devices_all, slots))
    face_source = jnp.zeros((devices_all, slots), jnp.int32).at[rows, orders].set(by_position)
    return (face_source.reshape(-1), face_send, mort_owner, mort_child)


def draw_face_source(key, part):
    return build_lists(key)[0]


def draw_face_send(key, part):
    return build_lists(key)[1]


def draw_mort_owner(key, part):
    return build_lists(key)[2]


def draw_mort_child(key, part):
    return build_lists(key)[3]


def touch_ends(entries, rng, smallest, largest):
    spot = [jax.random.randint(jax.random.fold_in(rng, axis), (), 0, length) for axis, length in enumerate(entries.shape)]
    widest = entries.shape.index(max(entries.shape))
    next_to = spot[:widest] + [(spot[widest] + 1) % entries.shape[widest]] + spot[widest + 1:]
    return entries.at[tuple(spot)].set(smallest).at[tuple(next_to)].set(largest)


def shard_levels(own_key, dims, pieces, least, high):
    def one(dim, blocks):
        steps = jax.random.uniform(jax.random.fold_in(jax.random.fold_in(own_key, 6), dim), (blocks,), jnp.float32, least / len(pieces), high / len(pieces))
        return jnp.repeat(jnp.exp(steps), dims[dim] // blocks).reshape((-1,) + (1,) * (len(dims) - dim - 1))

    gain = one(*pieces[0])
    for cut in pieces[1:]:
        gain = gain * one(*cut)
    return gain


def gaussian(key, dims, spread, limit, cuts=(), kind=jnp.bfloat16):
    gain = shard_levels(key, dims, cuts, -0.22, 0.18) if cuts else 1.0
    values = jax.random.normal(key, dims, jnp.float32) * spread * gain
    return jnp.minimum(jnp.maximum(values, -limit), limit).astype(kind)


def setup_inputs(seed: int = 0) -> dict:
    streams_of = jax.random.split(jax.random.key(seed), 9)
    return {
        "state": gaussian(streams_of[0], (ELEMS, FIELDS, NODES), 1.0, 6.0, ((0, 512),), jnp.float32),
        "levels": touch_ends(jax.random.randint(streams_of[1], (ELEMS,), 0, 3), jax.random.fold_in(streams_of[1], 1), 0, 2).astype(jnp.int32),
        "face_source": draw_face_source(jax.random.fold_in(streams_of[8], 71), 0),
        "face_send": draw_face_send(jax.random.fold_in(streams_of[8], 71), 0),
        "mort_owner": draw_mort_owner(jax.random.fold_in(streams_of[8], 71), 0),
        "mort_child": draw_mort_child(jax.random.fold_in(streams_of[8], 71), 0),
        "flux_jac": gaussian(streams_of[6], (3, FIELDS, FIELDS), 0.3, 1.75, (), jnp.float32),
        "penalty": jnp.clip(jax.random.uniform(streams_of[7], (FIELDS,), jnp.float32, 0.5, 1.5), 0.5, 1.5),
    }


OFFSETS = (-2, -1, 1, 2)
step_size = 0.01


def basis_tables(order):
    per_dim = order + 1
    eye_small = np.eye(per_dim)
    points = -np.cos(np.pi * np.arange(per_dim) / order)
    differences = points[:, None] - points[None, :] + eye_small
    barycentric = 1.0 / np.prod(differences, axis=1)
    derivative = (barycentric[None, :] / barycentric[:, None]) / differences
    derivative = np.where(eye_small > 0, 0.0, derivative)
    derivative = derivative - eye_small * derivative.sum(axis=1)[:, None]
    angles = np.pi * np.arange(per_dim) / order
    weights = np.ones(per_dim)
    for wave in range(1, order // 2 + 1):
        factor = 1.0 if 2 * wave == order else 2.0
        weights = weights - factor * np.cos(2.0 * wave * angles) / (4.0 * wave * wave - 1.0)
    edge_factor = np.where((np.arange(per_dim) == 0) | (np.arange(per_dim) == order), 1.0, 2.0)
    weights = edge_factor * weights / order

    def lagrange(targets):
        values_at = np.ones((per_dim, per_dim))
        for column in range(per_dim):
            for other in range(per_dim):
                if other != column:
                    values_at[:, column] *= (targets - points[other]) / (points[column] - points[other])
        return values_at

    halves = [lagrange((points - 1.0) / 2.0), lagrange((points + 1.0) / 2.0)]
    identity = np.eye(per_dim)
    deriv_mats = np.stack([np.kron(np.kron(derivative, identity), identity).T,
                           np.kron(np.kron(identity, derivative), identity).T,
                           np.kron(np.kron(identity, identity), derivative).T])
    node_index = np.arange(per_dim ** 3).reshape(per_dim, per_dim, per_dim)
    fnodes = per_dim * per_dim
    select = np.zeros((per_dim ** 3, 6 * fnodes))
    for face in range(6):
        ending = 0 if face % 2 == 0 else order
        picker = [slice(None), slice(None), slice(None)]
        picker[face // 2] = ending
        on_face = node_index[tuple(picker)].reshape(-1)
        select[on_face, face * fnodes + np.arange(fnodes)] = 1.0
    lift_mat = select.T / weights[0]
    face_weight = np.kron(weights, weights)
    proj = np.stack([np.kron(halves[quad // 2], halves[quad % 2]) for quad in range(4)])
    restrict = np.stack([0.25 * (proj[quad].T * face_weight[None, :]) / face_weight[:, None] for quad in range(4)])
    return (jnp.asarray(deriv_mats, jnp.float32), jnp.asarray(select, jnp.float32), jnp.asarray(lift_mat, jnp.float32),
            jnp.asarray(proj, jnp.float32), jnp.asarray(restrict, jnp.float32))


def project(large, proj):
    peers, pairs, width = large.shape
    fnodes = proj.shape[1]
    parts = large.reshape(peers, pairs, width // fnodes, fnodes)
    onto = jnp.einsum("pkfm,qnm->pkqfn", parts, proj, precision=lax.Precision.HIGHEST)
    return onto.reshape(peers, pairs * 4, width)


def restrict_sum(jumps, restrict):
    peers, quads, width = jumps.shape
    fnodes = restrict.shape[1]
    parts = jumps.reshape(peers, quads // 4, 4, width // fnodes, fnodes)
    back = jnp.einsum("pkqfn,qmn->pkfm", parts, restrict, precision=lax.Precision.HIGHEST)
    return -back.reshape(peers, quads // 4, width)


def add_rows(jump, index, values):
    target = jnp.where(index < 0, jump.shape[0], index)
    return jump.at[target].add(values, mode="drop")


def element_rhs(block, level_block, jump, deriv_mats, lift_mat, flux_jac, penalty):
    highest = lax.Precision.HIGHEST
    elements, fields, per_node = block.shape
    fnodes = lift_mat.shape[0] // 6
    flat = block.reshape(elements * fields, per_node)
    grads = jnp.stack([jnp.dot(flat, deriv_mats[direction], precision=highest) for direction in range(3)])
    grads = grads.reshape(3, elements, fields, per_node)
    volume = jnp.einsum("dgh,dehn->egn", flux_jac, grads, precision=highest)
    signs = jnp.array([-1.0, 1.0, -1.0, 1.0, -1.0, 1.0], jnp.float32)
    normal_jac = signs[:, None, None] * jnp.repeat(flux_jac, 2, axis=0)
    faces = jump.reshape(elements, 6, fields, fnodes)
    surface = 0.5 * (jnp.einsum("tgh,ethn->etgn", normal_jac, faces, precision=highest) - penalty[None, None, :, None] * faces)
    lifted = jnp.dot(surface.transpose(0, 2, 1, 3).reshape(elements * fields, 6 * fnodes), lift_mat, precision=highest)
    lifted = lifted.reshape(elements, fields, per_node)
    scale = jnp.exp2(level_block.astype(jnp.float32))
    return step_size * scale[:, None, None] * (lifted - volume)


def gather_masked(traces, index):
    rows = jnp.take_along_axis(traces, jnp.maximum(index, 0)[:, :, None], axis=1)
    return jnp.where(index[:, :, None] >= 0, rows, 0.0)


def reference(state, levels, face_source, face_send, mort_owner, mort_child, flux_jac, penalty):
    deriv_mats, select, lift_mat, proj, restrict = basis_tables(P_SIZE)
    highest = lax.Precision.HIGHEST
    devices_all = N_GX * N_GY
    slots = 6 * E_DEV
    values = jnp.dot(state.reshape(ELEMS * FIELDS, NODES), select, precision=highest)
    traces = values.reshape(ELEMS, FIELDS, 6, FNODES).transpose(0, 2, 1, 3).reshape(devices_all, slots, TRACE)
    outgoing = gather_masked(traces, face_send.reshape(devices_all, 4 * CAP)).reshape(devices_all, 4, CAP, TRACE)
    arrived = jnp.stack([jnp.roll(outgoing[:, place], OFFSETS[place], axis=0) for place in range(4)], axis=1)
    table_all = jnp.concatenate([traces, arrived.reshape(devices_all, 4 * CAP, TRACE)], axis=1)
    sources = face_source.reshape(devices_all, slots)
    neighbour = jnp.take_along_axis(table_all, jnp.maximum(sources, 0)[:, :, None], axis=1)
    jump = jnp.where(sources[:, :, None] >= 0, traces - neighbour, 0.0)
    owner_idx = mort_owner.reshape(devices_all, N_GY * MORT_PAIR)
    child_idx = mort_child.reshape(devices_all, N_GY * MCAP)
    large = gather_masked(traces, owner_idx).reshape(devices_all * N_GY, MORT_PAIR, TRACE)
    small = gather_masked(traces, child_idx).reshape(N_GX, N_GY, N_GY, MCAP, TRACE)
    small = small.transpose(0, 2, 1, 3, 4).reshape(devices_all * N_GY, MCAP, TRACE)
    mjump = small - project(large, proj)
    back = restrict_sum(mjump, restrict)
    child_add = mjump.reshape(N_GX, N_GY, N_GY, MCAP, TRACE).transpose(0, 2, 1, 3, 4).reshape(devices_all, N_GY * MCAP, TRACE)
    jump = jax.vmap(add_rows)(jump, child_idx, child_add)
    jump = jax.vmap(add_rows)(jump, owner_idx, back.reshape(devices_all, N_GY * MORT_PAIR, TRACE))
    blocks = state.reshape(devices_all, E_DEV, FIELDS, NODES)
    level_blocks = levels.reshape(devices_all, E_DEV)

    def one_device(parts):
        return element_rhs(parts[0], parts[1], parts[2], deriv_mats, lift_mat, flux_jac, penalty)

    result = lax.map(one_device, (blocks, level_blocks, jump))
    return result.reshape(ELEMS, FIELDS, NODES)
```

```python
import jax
import jax.numpy as jnp
import ml_dtypes
import numpy as np
from jax import lax
from jax.experimental import pallas as pl
from jax.experimental.pallas import tpu as pltpu
from jax.sharding import PartitionSpec as P

P_SIZE = 7
OFFSETS = (-2, -1, 1, 2)
STEP_SIZE = 0.01

F32 = jnp.float32
BF16 = jnp.bfloat16
HIGHEST = lax.Precision.HIGHEST
VMEM = pl.BlockSpec(memory_space=pltpu.VMEM)
SMEM = pl.BlockSpec(memory_space=pltpu.SMEM)
MIB = 1 << 20


def shifted(value, axis, steps):
    count = lax.axis_size(axis)
    pairs = [(source, (source + steps) % count) for source in range(count)]
    return lax.ppermute(value, axis, pairs)


def pieces_of(table):
    rest = np.asarray(table, np.float32)
    out = []
    for _ in range(3):
        piece = rest.astype(ml_dtypes.bfloat16)
        out.append(piece)
        rest = rest - piece.astype(np.float32)
    return np.stack(out)


def basis_tables(order):
    per_dim = order + 1
    eye_small = np.eye(per_dim)
    points = -np.cos(np.pi * np.arange(per_dim) / order)
    differences = points[:, None] - points[None, :] + eye_small
    barycentric = 1.0 / np.prod(differences, axis=1)
    derivative = barycentric[None, :] / barycentric[:, None] / differences
    derivative = np.where(eye_small > 0, 0.0, derivative)
    derivative = derivative - eye_small * derivative.sum(axis=1)[:, None]
    angles = np.pi * np.arange(per_dim) / order
    weights = np.ones(per_dim)
    for wave in range(1, order // 2 + 1):
        factor = 1.0 if 2 * wave == order else 2.0
        weights = weights - factor * np.cos(2.0 * wave * angles) / (4.0 * wave * wave - 1.0)
    edge_factor = np.where((np.arange(per_dim) == 0) | (np.arange(per_dim) == order), 1.0, 2.0)
    weights = edge_factor * weights / order

    def lagrange(targets):
        values_at = np.ones((per_dim, per_dim))
        for column in range(per_dim):
            for other in range(per_dim):
                if other != column:
                    values_at[:, column] *= (targets - points[other]) / (
                        points[column] - points[other]
                    )
        return values_at

    halves = [lagrange((points - 1.0) / 2.0), lagrange((points + 1.0) / 2.0)]
    identity = np.eye(per_dim)
    node_index = np.arange(per_dim**3).reshape(per_dim, per_dim, per_dim)
    fnodes = per_dim * per_dim
    select = np.zeros((per_dim**3, 4 * fnodes), np.float32)
    for face in range(2, 6):
        picker = [slice(None), slice(None), slice(None)]
        picker[face // 2] = 0 if face % 2 == 0 else order
        on_face = node_index[tuple(picker)].reshape(-1)
        select[on_face, (face - 2) * fnodes + np.arange(fnodes)] = 1.0
    face_weight = np.kron(weights, weights)
    proj = [np.kron(halves[quad // 2], halves[quad % 2]) for quad in range(4)]
    restrict = [
        0.25 * (proj[quad].T * face_weight[None, :]) / face_weight[:, None] for quad in range(4)
    ]
    two = np.eye(2)
    both = sum(restrict[quad] @ proj[quad] for quad in range(4))
    quarter = np.eye(4)
    return {
        "select": select.astype(ml_dtypes.bfloat16),
        "lift": np.ascontiguousarray(select.T).astype(ml_dtypes.bfloat16),
        "restrict": np.concatenate([np.kron(two, r.T) for r in restrict], 0).astype(np.float32),
        "project": np.concatenate([np.kron(two, p.T) for p in proj], 1).astype(np.float32),
        "both": np.kron(two, both.T).astype(np.float32),
        "deriv_0": pieces_of(np.kron(derivative, np.eye(fnodes)).T),
        "deriv_1": pieces_of(np.kron(quarter, np.kron(derivative, identity)).T),
        "deriv_2": pieces_of(np.kron(quarter, np.kron(identity, derivative)).T),
        "edge": float(1.0 / weights[0]),
    }


def split3(value):
    high = value.astype(BF16)
    rest = value - high.astype(F32)
    middle = rest.astype(BF16)
    low = (rest - middle.astype(F32)).astype(BF16)
    return high, middle, low


def mm(a, b):
    return jnp.dot(a, b, preferred_element_type=F32)


def low_half(rows):
    return lax.broadcasted_iota(jnp.int32, (rows, 128), 1) < 64


def swap_halves(value):
    return pltpu.roll(value, 64, 1)


def column_of(row):
    count = row.shape[1]
    spread = jnp.broadcast_to(row.astype(F32), (count, count))
    down = lax.broadcasted_iota(jnp.int32, (count, count), 0)
    across = lax.broadcasted_iota(jnp.int32, (count, count), 1)
    return jnp.sum(jnp.where(down == across, spread, 0.0), axis=1, keepdims=True).astype(jnp.int32)


def slot_row(count):
    at = lax.broadcasted_iota(jnp.int32, (1, count), 1)
    return 6 * (at % 128) + at // 128


def pre_kernel(
    state, send, owner, child, select, restrict, s0, s1, s2, s3, mort, table, large, small
):
    low = low_half(128)
    for pair in range(3):
        fields = [split3(state[2 * pair + side]) for side in range(2)]
        lanes = slice(128 * pair, 128 * pair + 128)
        for piece in range(3):
            even, odd = fields[0][piece], fields[1][piece]
            even_on, odd_on = mm(even, select[...]), mm(odd, select[...])
            first = [even[:, :128].astype(F32), even_on[:, :128], even_on[:, 128:]]
            first_odd = [odd[:, :128].astype(F32), odd_on[:, :128], odd_on[:, 128:]]
            last = [even[:, 384:].astype(F32), even_on[:, :128], even_on[:, 128:]]
            last_odd = [odd[:, 384:].astype(F32), odd_on[:, :128], odd_on[:, 128:]]
            for dim in range(3):
                front = jnp.where(low, first[dim], swap_halves(first_odd[dim]))
                back = jnp.where(low, swap_halves(last[dim]), last_odd[dim])
                table[piece, 256 * dim : 256 * dim + 128, lanes] = front.astype(BF16)
                table[piece, 256 * dim + 128 : 256 * dim + 256, lanes] = back.astype(BF16)
    slots = slot_row(768)
    index = [column_of(send[o : o + 1, :]) for o in range(4)]
    index.append(column_of(owner[...]))
    index += [column_of(child[q : q + 1, :]) for q in range(4)]
    pick = jnp.where(jnp.concatenate(index, 0) == slots, 1.0, 0.0).astype(BF16)
    rows = mm(pick, table[0]) + mm(pick, table[1]) + mm(pick, table[2])
    for o, out in enumerate((s0, s1, s2, s3)):
        out[...] = rows[32 * o : 32 * o + 32]
    large[...] = rows[128:160]
    small[...] = rows[160:288]
    stacked = jnp.concatenate(
        [
            jnp.concatenate(
                [
                    rows[160 + 32 * q : 192 + 32 * q, 128 * part : 128 * part + 128]
                    for q in range(4)
                ],
                1,
            )
            for part in range(3)
        ],
        0,
    )
    back = jnp.dot(stacked, restrict[...], precision=HIGHEST, preferred_element_type=F32)
    for part in range(3):
        mort[pl.ds(part, 32, stride=8), :] = back[32 * part : 32 * part + 32]
        mort[pl.ds(3 + part, 32, stride=8), :] = rows[128:160, 128 * part : 128 * part + 128]
    for part in (6, 7):
        mort[pl.ds(part, 32, stride=8), :] = jnp.zeros((32, 128), F32)


def mid_kernel(
    state, table, source, levels, owner, child, large, both, d0, d1, d2, flux,
    local, remote, own_back, minus_volume,
):
    level = column_of(levels[...])
    twos = (1 << level).astype(F32)
    slots = slot_row(768)
    element = lax.broadcasted_iota(jnp.int32, (128, 1), 0)
    diagonal = lax.broadcasted_iota(
        jnp.int32, (128, 128), 0
    ) == lax.broadcasted_iota(jnp.int32, (128, 128), 1)
    arrived_slot = 768 + lax.broadcasted_iota(jnp.int32, (1, 128), 1)
    child_row = jnp.concatenate([child[q : q + 1, :] for q in range(4)], 1)
    owner_row = owner[...]
    for face in range(6):
        wanted = source[:, face : face + 1]
        mine = 6 * element + face
        rows = slice(128 * face, 128 * face + 128)
        minus = -twos
        blocks = []
        for other in range(6):
            block = jnp.where(wanted == slots[:, 128 * other : 128 * other + 128], minus, 0.0)
            if other == face:
                block = block + jnp.where(diagonal & (wanted >= 0), twos, 0.0)
            blocks.append(block.astype(BF16))
        matrix = jnp.concatenate(blocks, 1)
        local[rows, :] = mm(matrix, table[0]) + mm(matrix, table[1]) + mm(matrix, table[2])
        remote[rows, 0:128] = jnp.where(wanted == arrived_slot, minus, 0.0).astype(BF16)
        remote[rows, 128:256] = jnp.where(mine == child_row, minus, 0.0).astype(BF16)
        remote[rows, 256:288] = jnp.where(mine == owner_row, minus, 0.0).astype(BF16)
    for part in range(3):
        own_back[:, 128 * part : 128 * part + 128] = jnp.dot(
            large[:, 128 * part : 128 * part + 128],
            both[...],
            precision=HIGHEST,
            preferred_element_type=F32,
        )

    def apply(parts, matrix):
        high, middle, low = parts
        small = mm(high, matrix[2]) + mm(middle, matrix[1]) + mm(low, matrix[0])
        return mm(high, matrix[0]) + (mm(high, matrix[1]) + mm(middle, matrix[0]) + small)

    amount = -STEP_SIZE * twos
    grads = []
    for field in range(6):
        parts = split3(state[field])
        along = [apply(parts, d0)]
        for matrix in (d1, d2):
            along.append(
                jnp.concatenate(
                    [apply([p[:, 256 * h : 256 * h + 256] for p in parts], matrix) for h in range(2)],
                    1,
                )
            )
        grads.append(along)
    for out in range(6):
        total = 0.0
        for dim in range(3):
            for field in range(6):
                total = total + flux[dim, out, field] * grads[field][dim]
        minus_volume[out] = amount * total


def post_kernel(
    local, remote, minus_volume, a0, a1, a2, a3, got, small, own_back, project, lift, flux,
    penalty, edge, out,
):
    got_back = [got[pl.ds(part, 32, stride=8), :] for part in range(3)]
    got_large = [got[pl.ds(3 + part, 32, stride=8), :] for part in range(3)]
    onto = jnp.dot(
        jnp.concatenate(got_large, 0), project[...], precision=HIGHEST, preferred_element_type=F32
    )
    child = jnp.concatenate(
        [
            jnp.concatenate(
                [
                    onto[32 * part : 32 * part + 32, 128 * q : 128 * q + 128]
                    for part in range(3)
                ],
                1,
            )
            for q in range(4)
        ],
        0,
    )
    extra = jnp.concatenate(
        [
            a0[...],
            a1[...],
            a2[...],
            a3[...],
            child - small[...],
            jnp.concatenate(got_back, 1) - own_back[...],
        ],
        0,
    )
    parts = split3(extra)
    factor = 0.5 * STEP_SIZE * edge
    low = low_half(128)
    signs = jnp.where(low, -1.0, 1.0)
    surface = [[None] * 3 for _ in range(6)]
    for dim in range(3):
        ends = []
        for side in range(2):
            rows = slice(256 * dim + 128 * side, 256 * dim + 128 * side + 128)
            matrix = remote[rows, :]
            far = mm(matrix, parts[0]) + mm(matrix, parts[1]) + mm(matrix, parts[2])
            ends.append(local[rows, :] + far)
        jumps = []
        for pair in range(3):
            lanes = slice(128 * pair, 128 * pair + 128)
            front, back = ends[0][:, lanes], ends[1][:, lanes]
            jumps.append(jnp.where(low, front, swap_halves(back)))
            jumps.append(jnp.where(low, swap_halves(front), back))
        for field in range(6):
            mixed = (factor * flux[dim, field, 0]) * jumps[0]
            for other in range(1, 6):
                mixed = mixed + (factor * flux[dim, field, other]) * jumps[other]
            surface[field][dim] = signs * mixed - (factor * penalty[field]) * jumps[field]
    for field in range(6):
        lifted = 0.0
        for piece in split3(jnp.concatenate(surface[field][1:], 1)):
            lifted = lifted + mm(piece, lift[...])
        ends = surface[field][0]
        total = minus_volume[field] + lifted
        out[field, :, 0:128] = total[:, 0:128] + jnp.where(low, ends, 0.0)
        out[field, :, 128:384] = total[:, 128:384]
        out[field, :, 384:512] = total[:, 384:512] + jnp.where(low, 0.0, ends)


def per_device(state, levels, face_source, face_send, mort_owner, mort_child, flux_jac, penalty):
    tables = basis_tables(P_SIZE)
    fields_first = state.transpose(1, 0, 2)
    send = face_send.reshape(4, 32)
    owner = mort_owner.reshape(1, 32)
    child = mort_child.transpose(0, 2, 1).reshape(4, 32)

    def shape(dims, kind=F32):
        return jax.ShapeDtypeStruct(dims, kind)

    params = pltpu.CompilerParams(vmem_limit_bytes=28 * MIB)
    s0, s1, s2, s3, mort, table, large, small = pl.pallas_call(
        pre_kernel,
        out_shape=[shape((32, 384))] * 4
        + [
            shape((256, 128)),
            shape((3, 768, 384), BF16),
            shape((32, 384)),
            shape((128, 384)),
        ],
        in_specs=[VMEM] * 6,
        out_specs=[VMEM] * 8,
        compiler_params=params,
        cost_estimate=pl.CostEstimate(flops=10**9, bytes_accessed=4 << 20, transcendentals=0),
        name="pre",
    )(fields_first, send, owner, child, tables["select"], tables["restrict"])
    arrived = [
        shifted(rows, ("gx", "gy"), OFFSETS[place]) for place, rows in enumerate((s0, s1, s2, s3))
    ]
    got = lax.all_to_all(mort.reshape(32, 8, 128), "gy", split_axis=0, concat_axis=0, tiled=True)
    local, remote, own_back, minus_volume = pl.pallas_call(
        mid_kernel,
        out_shape=[
            shape((768, 384)),
            shape((768, 288), BF16),
            shape((32, 384)),
            shape((6, 128, 512)),
        ],
        in_specs=[VMEM] * 11 + [SMEM],
        out_specs=[VMEM] * 4,
        compiler_params=params,
        cost_estimate=pl.CostEstimate(flops=8 * 10**9, bytes_accessed=8 << 20, transcendentals=0),
        name="mid",
    )(
        fields_first,
        table,
        face_source.reshape(128, 6),
        levels.reshape(1, 128),
        owner,
        child,
        large,
        tables["both"],
        tables["deriv_0"],
        tables["deriv_1"],
        tables["deriv_2"],
        flux_jac,
    )
    edge = tables["edge"]

    def post(*refs):
        post_kernel(*refs[:14], edge, refs[14])

    result = pl.pallas_call(
        post,
        out_shape=shape((6, 128, 512)),
        in_specs=[VMEM] * 12 + [SMEM] * 2,
        out_specs=VMEM,
        compiler_params=params,
        cost_estimate=pl.CostEstimate(flops=2 * 10**9, bytes_accessed=4 << 20, transcendentals=0),
        name="post",
    )(
        local,
        remote,
        minus_volume,
        *arrived,
        got.reshape(256, 128),
        small,
        own_back,
        tables["project"],
        tables["lift"],
        flux_jac,
        penalty,
    )
    return result.transpose(1, 0, 2)


def solution(mesh):
    in_specs = (
        P(("gx", "gy"), None, None),
        P(("gx", "gy")),
        P(("gx", "gy")),
        P(("gx", "gy"), None, None),
        P(("gx", "gy"), None, None),
        P(("gx", "gy"), None, None),
        P(),
        P(),
    )
    out_specs = P(("gx", "gy"), None, None)
    return jax.shard_map(
        per_device, mesh=mesh, in_specs=in_specs, out_specs=out_specs, check_vma=False
    )
```

```python
import jax
import jax.numpy as jnp
import ml_dtypes
import numpy as np
from jax import lax
from jax.experimental import pallas as pl
from jax.experimental.pallas import tpu as pltpu
from jax.sharding import PartitionSpec as P

P_SIZE = 7
OFFSETS = (-2, -1, 1, 2)
STEP_SIZE = 0.01

F32 = jnp.float32
BF16 = jnp.bfloat16
HIGHEST = lax.Precision.HIGHEST
VMEM = pl.BlockSpec(memory_space=pltpu.VMEM)
HBM = pl.BlockSpec(memory_space=pltpu.HBM)
SMEM = pl.BlockSpec(memory_space=pltpu.SMEM)
MIB = 1 << 20


def shifted(value, axis, steps):
    count = lax.axis_size(axis)
    pairs = [(source, (source + steps) % count) for source in range(count)]
    return lax.ppermute(value, axis, pairs)


def pieces_of(table):
    rest = np.asarray(table, np.float32)
    out = []
    for _ in range(2):
        piece = rest.astype(ml_dtypes.bfloat16)
        out.append(piece)
        rest = rest - piece.astype(np.float32)
    return np.stack(out)


def basis_tables(order):
    per_dim = order + 1
    eye_small = np.eye(per_dim)
    points = -np.cos(np.pi * np.arange(per_dim) / order)
    differences = points[:, None] - points[None, :] + eye_small
    barycentric = 1.0 / np.prod(differences, axis=1)
    derivative = barycentric[None, :] / barycentric[:, None] / differences
    derivative = np.where(eye_small > 0, 0.0, derivative)
    derivative = derivative - eye_small * derivative.sum(axis=1)[:, None]
    angles = np.pi * np.arange(per_dim) / order
    weights = np.ones(per_dim)
    for wave in range(1, order // 2 + 1):
        factor = 1.0 if 2 * wave == order else 2.0
        weights = weights - factor * np.cos(2.0 * wave * angles) / (4.0 * wave * wave - 1.0)
    edge_factor = np.where((np.arange(per_dim) == 0) | (np.arange(per_dim) == order), 1.0, 2.0)
    weights = edge_factor * weights / order

    def lagrange(targets):
        values_at = np.ones((per_dim, per_dim))
        for column in range(per_dim):
            for other in range(per_dim):
                if other != column:
                    values_at[:, column] *= (targets - points[other]) / (
                        points[column] - points[other]
                    )
        return values_at

    halves = [lagrange((points - 1.0) / 2.0), lagrange((points + 1.0) / 2.0)]
    identity = np.eye(per_dim)
    node_index = np.arange(per_dim**3).reshape(per_dim, per_dim, per_dim)
    fnodes = per_dim * per_dim
    select = np.zeros((per_dim**3, 4 * fnodes), np.float32)
    for face in range(2, 6):
        picker = [slice(None), slice(None), slice(None)]
        picker[face // 2] = 0 if face % 2 == 0 else order
        on_face = node_index[tuple(picker)].reshape(-1)
        select[on_face, (face - 2) * fnodes + np.arange(fnodes)] = 1.0
    face_weight = np.kron(weights, weights)
    proj = [np.kron(halves[quad // 2], halves[quad % 2]) for quad in range(4)]
    restrict = [
        0.25 * (proj[quad].T * face_weight[None, :]) / face_weight[:, None] for quad in range(4)
    ]
    two = np.eye(2)
    both = sum(restrict[quad] @ proj[quad] for quad in range(4))
    quarter = np.eye(4)
    return {
        "select": select.astype(ml_dtypes.bfloat16),
        "lift": np.ascontiguousarray(select.T).astype(ml_dtypes.bfloat16),
        "restrict": np.concatenate([np.kron(two, r.T) for r in restrict], 0).astype(np.float32),
        "project": np.concatenate([np.kron(two, p.T) for p in proj], 1).astype(np.float32),
        "both": np.kron(two, both.T).astype(np.float32),
        "deriv_0": pieces_of(np.kron(derivative, np.eye(fnodes)).T),
        "deriv_1": pieces_of(np.kron(quarter, np.kron(derivative, identity)).T),
        "deriv_2": pieces_of(np.kron(quarter, np.kron(identity, derivative)).T),
        "edge": float(1.0 / weights[0]),
    }


def split3(value):
    high = value.astype(BF16)
    rest = value - high.astype(F32)
    middle = rest.astype(BF16)
    low = (rest - middle.astype(F32)).astype(BF16)
    return high, middle, low


def mm(a, b):
    return jnp.dot(a, b, preferred_element_type=F32)


def low_half(rows):
    return lax.broadcasted_iota(jnp.int32, (rows, 128), 1) < 64


def swap_halves(value):
    return pltpu.roll(value, 64, 1)


def column_of(row):
    count = row.shape[1]
    spread = jnp.broadcast_to(row.astype(F32), (count, count))
    down = lax.broadcasted_iota(jnp.int32, (count, count), 0)
    across = lax.broadcasted_iota(jnp.int32, (count, count), 1)
    return jnp.sum(jnp.where(down == across, spread, 0.0), axis=1, keepdims=True).astype(jnp.int32)


def slot_row(count):
    at = lax.broadcasted_iota(jnp.int32, (1, count), 1)
    return 6 * (at % 128) + at // 128


def start_all(sources, targets, arrivals):
    copies = [
        pltpu.make_async_copy(source, target, arrivals.at[at])
        for at, (source, target) in enumerate(zip(sources, targets, strict=True))
    ]
    for copy in copies:
        copy.start()
    return copies


def rows_of(field):
    return slice(128 * field, 128 * field + 128)


def pre_kernel(
    state_far, send_far, owner_far, child_far, select_far, restrict_far,
    s0_far, s1_far, s2_far, s3_far, mort_far, table_far, large_far, small_far,
    state, send, owner, child, select, restrict, ends, pieces, table, picked, mort, arrivals, sent,
):
    copies = start_all(
        [select_far, *(state_far.at[rows_of(f)] for f in range(6)), send_far, owner_far, child_far, restrict_far],
        [select, *(state.at[rows_of(f)] for f in range(6)), send, owner, child, restrict],
        arrivals,
    )
    low = low_half(128)
    for field in range(6):
        copies[1 + field].wait()
        rows = rows_of(field)
        for piece, value in enumerate(split3(state[rows])):
            pieces[piece, rows] = value
            ends[piece, rows, :128] = value[:, :128].astype(F32)
            ends[piece, rows, 128:] = value[:, 384:].astype(F32)
    copies[0].wait()
    for piece in range(3):
        inner = mm(pieces[piece], select[...])
        for pair in range(3):
            even, odd = rows_of(2 * pair), rows_of(2 * pair + 1)
            lanes = slice(128 * pair, 128 * pair + 128)
            fronts = [(ends[piece, even, :128], ends[piece, odd, :128])]
            backs = [(ends[piece, even, 128:], ends[piece, odd, 128:])]
            for dim in range(2):
                at = slice(128 * dim, 128 * dim + 128)
                fronts.append((inner[even, at], inner[odd, at]))
            backs += fronts[1:]
            for dim in range(3):
                front = jnp.where(low, fronts[dim][0], swap_halves(fronts[dim][1]))
                back = jnp.where(low, swap_halves(backs[dim][0]), backs[dim][1])
                table[piece, 256 * dim : 256 * dim + 128, lanes] = front.astype(BF16)
                table[piece, 256 * dim + 128 : 256 * dim + 256, lanes] = back.astype(BF16)
    leaving = start_all([table], [table_far], sent)
    for copy in copies[7:]:
        copy.wait()
    slots = slot_row(768)
    index = [column_of(send[o : o + 1, :]) for o in range(4)]
    index.append(column_of(owner[...]))
    index += [column_of(child[q : q + 1, :]) for q in range(4)]
    pick = jnp.where(jnp.concatenate(index, 0) == slots, 1.0, 0.0).astype(BF16)
    picked[...] = mm(pick, table[0]) + mm(pick, table[1]) + mm(pick, table[2])
    leaving += start_all(
        [*(picked.at[32 * o : 32 * o + 32] for o in range(4)), picked.at[128:160], picked.at[160:288]],
        [s0_far, s1_far, s2_far, s3_far, large_far, small_far],
        sent.at[1:7],
    )
    stacked = jnp.concatenate(
        [
            jnp.concatenate(
                [
                    picked[160 + 32 * q : 192 + 32 * q, 128 * part : 128 * part + 128]
                    for q in range(4)
                ],
                1,
            )
            for part in range(3)
        ],
        0,
    )
    back = jnp.dot(stacked, restrict[...], precision=HIGHEST, preferred_element_type=F32)
    for part in range(3):
        mort[pl.ds(part, 32, stride=8), :] = back[32 * part : 32 * part + 32]
        mort[pl.ds(3 + part, 32, stride=8), :] = picked[128:160, 128 * part : 128 * part + 128]
    for part in (6, 7):
        mort[pl.ds(part, 32, stride=8), :] = jnp.zeros((32, 128), F32)
    leaving += start_all([mort], [mort_far], sent.at[7:8])
    for copy in leaving:
        copy.wait()


def mid_kernel(
    levels_far, owner_far, child_far, source_far, state_far, d0_far, d1_far, d2_far, table_far,
    large_far, both_far, flux, local_far, remote_far, own_back_far, minus_volume_far,
    levels, owner, child, source, state, d0, d1, d2, table, large, both, local, remote, own_back,
    minus_volume, pieces, grads, matrix, amount, arrivals, sent,
):
    copies = start_all(
        [levels_far, owner_far, child_far, source_far, state_far, d0_far, d1_far, d2_far, table_far, large_far, both_far],
        [levels, owner, child, source, state, d0, d1, d2, table, large, both],
        arrivals,
    )
    for copy in copies[:4]:
        copy.wait()
    level = column_of(levels[...])
    twos = (1 << level).astype(F32)
    minus = -twos
    amount[...] = jnp.broadcast_to(minus * STEP_SIZE, (128, 128))
    slots = slot_row(768)
    element = lax.broadcasted_iota(jnp.int32, (128, 1), 0)
    diagonal = lax.broadcasted_iota(
        jnp.int32, (128, 128), 0
    ) == lax.broadcasted_iota(jnp.int32, (128, 128), 1)
    arrived_slot = 768 + lax.broadcasted_iota(jnp.int32, (1, 128), 1)
    child_row = jnp.concatenate([child[q : q + 1, :] for q in range(4)], 1)
    owner_row = owner[...]
    for face in range(6):
        wanted = source[:, face : face + 1]
        mine = 6 * element + face
        rows = rows_of(face)
        for other in range(6):
            block = jnp.where(wanted == slots[:, rows_of(other)], minus, 0.0)
            if other == face:
                block = block + jnp.where(diagonal & (wanted >= 0), twos, 0.0)
            matrix[rows, rows_of(other)] = block.astype(BF16)
        remote[rows, 0:128] = jnp.where(wanted == arrived_slot, minus, 0.0).astype(BF16)
        remote[rows, 128:256] = jnp.where(mine == child_row, minus, 0.0).astype(BF16)
        remote[rows, 256:288] = jnp.where(mine == owner_row, minus, 0.0).astype(BF16)
    leaving = start_all([remote], [remote_far], sent)
    copies[4].wait()
    for field in range(6):
        rows = rows_of(field)
        value = state[rows]
        high = value.astype(BF16)
        pieces[0, rows] = high
        pieces[1, rows] = (value - high.astype(F32)).astype(BF16)
    for copy in copies[5:8]:
        copy.wait()

    def apply(lanes, deriv):
        high, rest = pieces[0, :, lanes], pieces[1, :, lanes]
        return mm(high, deriv[0]) + (mm(high, deriv[1]) + mm(rest, deriv[0]))

    grads[0] = apply(slice(0, 512), d0)
    for half in range(2):
        lanes = slice(256 * half, 256 * half + 256)
        grads[1, :, lanes] = apply(lanes, d1)
        grads[2, :, lanes] = apply(lanes, d2)

    def mix(step, carry):
        first = pl.multiple_of(8 * step, 8)
        scale = amount[pl.ds(first, 8), :]
        scale = jnp.concatenate([scale, scale], 1)
        for half in range(2):
            lanes = slice(256 * half, 256 * half + 256)
            parts = [
                [grads[dim, pl.ds(128 * field + first, 8), lanes] for field in range(6)]
                for dim in range(3)
            ]
            for out in range(6):
                total = flux[0, out, 0] * parts[0][0]
                for dim in range(3):
                    for field in range(6):
                        if dim + field:
                            total = total + flux[dim, out, field] * parts[dim][field]
                minus_volume[pl.ds(128 * out + first, 8), lanes] = scale * total
        return carry

    lax.fori_loop(0, 16, mix, 0)
    leaving += start_all([minus_volume], [minus_volume_far], sent.at[1:2])
    for copy in copies[8:]:
        copy.wait()
    local[...] = (
        mm(matrix[...], table[0]) + mm(matrix[...], table[1]) + mm(matrix[...], table[2])
    )
    leaving += start_all([local], [local_far], sent.at[2:3])
    for part in range(3):
        own_back[:, 128 * part : 128 * part + 128] = jnp.dot(
            large[:, 128 * part : 128 * part + 128],
            both[...],
            precision=HIGHEST,
            preferred_element_type=F32,
        )
    leaving += start_all([own_back], [own_back_far], sent.at[3:4])
    for copy in leaving:
        copy.wait()


def post_kernel(
    got_far, project_far, a0_far, a1_far, a2_far, a3_far, small_far, own_back_far, remote_far,
    local_far, lift_far, minus_volume_far, flux, penalty, edge, out_far,
    got, project, arrived, small, own_back, remote, local, lift, minus_volume,
    jumps, ends, pieces, out, arrivals, done,
):
    copies = start_all(
        [got_far, project_far, a0_far, a1_far, a2_far, a3_far, small_far, own_back_far, remote_far, local_far, lift_far, minus_volume_far],
        [got, project, *(arrived.at[32 * o : 32 * o + 32] for o in range(4)), small, own_back, remote, local, lift, minus_volume],
        arrivals,
    )
    for copy in copies[:8]:
        copy.wait()
    got_back = [got[pl.ds(part, 32, stride=8), :] for part in range(3)]
    got_large = [got[pl.ds(3 + part, 32, stride=8), :] for part in range(3)]
    onto = jnp.dot(
        jnp.concatenate(got_large, 0), project[...], precision=HIGHEST, preferred_element_type=F32
    )
    child = jnp.concatenate(
        [
            jnp.concatenate(
                [
                    onto[32 * part : 32 * part + 32, 128 * q : 128 * q + 128]
                    for part in range(3)
                ],
                1,
            )
            for q in range(4)
        ],
        0,
    )
    extra = jnp.concatenate(
        [
            arrived[...],
            child - small[...],
            jnp.concatenate(got_back, 1) - own_back[...],
        ],
        0,
    )
    parts = split3(extra)
    copies[8].wait()
    copies[9].wait()
    picks = remote[...]
    jumps[...] = local[...] + (mm(picks, parts[0]) + mm(picks, parts[1]) + mm(picks, parts[2]))
    factor = 0.5 * STEP_SIZE * edge
    step = 16
    low = low_half(step)
    signs = jnp.where(low, -1.0, 1.0)
    for dim in range(3):
        rates = [[factor * flux[dim, g, h] for h in range(6)] for g in range(6)]
        drags = [factor * penalty[g] for g in range(6)]
        for first in range(0, 128, step):
            values = []
            for pair in range(3):
                lanes = slice(128 * pair, 128 * pair + 128)
                front = jumps[256 * dim + first : 256 * dim + first + step, lanes]
                back = jumps[256 * dim + 128 + first : 256 * dim + 128 + first + step, lanes]
                values.append(jnp.where(low, front, swap_halves(back)))
                values.append(jnp.where(low, swap_halves(front), back))
            for field in range(6):
                mixed = rates[field][0] * values[0]
                for other in range(1, 6):
                    mixed = mixed + rates[field][other] * values[other]
                surface = signs * mixed - drags[field] * values[field]
                rows = slice(128 * field + first, 128 * field + first + step)
                if dim == 0:
                    ends[rows] = surface
                else:
                    for piece, value in enumerate(split3(surface)):
                        pieces[piece, rows, 128 * dim - 128 : 128 * dim] = value
    copies[10].wait()
    copies[11].wait()
    low = low_half(256)
    sent = []
    for pair in range(3):
        rows = slice(256 * pair, 256 * pair + 256)
        lifted = mm(pieces[0, rows], lift[...])
        lifted = lifted + mm(pieces[1, rows], lift[...])
        lifted = lifted + mm(pieces[2, rows], lift[...])
        total = minus_volume[rows] + lifted
        edges = ends[rows]
        out[rows, 0:128] = total[:, 0:128] + jnp.where(low, edges, 0.0)
        out[rows, 128:384] = total[:, 128:384]
        out[rows, 384:512] = total[:, 384:512] + jnp.where(low, 0.0, edges)
        copy = pltpu.make_async_copy(out.at[rows], out_far.at[rows], done.at[pair])
        copy.start()
        sent.append(copy)
    for copy in sent:
        copy.wait()


def per_device(state, levels, face_source, face_send, mort_owner, mort_child, flux_jac, penalty):
    tables = basis_tables(P_SIZE)
    by_field = state.transpose(1, 0, 2).reshape(768, 512)
    send = face_send.reshape(4, 32)
    owner = mort_owner.reshape(1, 32)
    child = mort_child.transpose(0, 2, 1).reshape(4, 32)

    def shape(dims, kind=F32):
        return jax.ShapeDtypeStruct(dims, kind)

    params = pltpu.CompilerParams(vmem_limit_bytes=60 * MIB)
    s0, s1, s2, s3, mort, table, large, small = pl.pallas_call(
        pre_kernel,
        out_shape=[shape((32, 384))] * 4
        + [
            shape((256, 128)),
            shape((3, 768, 384), BF16),
            shape((32, 384)),
            shape((128, 384)),
        ],
        in_specs=[HBM] * 6,
        out_specs=[HBM] * 8,
        scratch_shapes=[
            pltpu.VMEM((768, 512), F32),
            pltpu.VMEM((4, 32), jnp.int32),
            pltpu.VMEM((1, 32), jnp.int32),
            pltpu.VMEM((4, 32), jnp.int32),
            pltpu.VMEM((512, 256), BF16),
            pltpu.VMEM((512, 128), F32),
            pltpu.VMEM((3, 768, 256), F32),
            pltpu.VMEM((3, 768, 512), BF16),
            pltpu.VMEM((3, 768, 384), BF16),
            pltpu.VMEM((288, 384), F32),
            pltpu.VMEM((256, 128), F32),
            pltpu.SemaphoreType.DMA((11,)),
            pltpu.SemaphoreType.DMA((8,)),
        ],
        compiler_params=params,
        cost_estimate=pl.CostEstimate(flops=10**9, bytes_accessed=4 << 20, transcendentals=0),
        name="pre",
    )(by_field, send, owner, child, tables["select"], tables["restrict"])
    arrived = [
        shifted(rows, ("gx", "gy"), OFFSETS[place]) for place, rows in enumerate((s0, s1, s2, s3))
    ]
    got = lax.all_to_all(mort.reshape(32, 8, 128), "gy", split_axis=0, concat_axis=0, tiled=True)
    local, remote, own_back, minus_volume = pl.pallas_call(
        mid_kernel,
        out_shape=[
            shape((768, 384)),
            shape((768, 288), BF16),
            shape((32, 384)),
            shape((768, 512)),
        ],
        in_specs=[HBM] * 11 + [SMEM],
        out_specs=[HBM] * 4,
        scratch_shapes=[
            pltpu.VMEM((1, 128), jnp.int32),
            pltpu.VMEM((1, 32), jnp.int32),
            pltpu.VMEM((4, 32), jnp.int32),
            pltpu.VMEM((128, 6), jnp.int32),
            pltpu.VMEM((768, 512), F32),
            pltpu.VMEM((2, 512, 512), BF16),
            pltpu.VMEM((2, 256, 256), BF16),
            pltpu.VMEM((2, 256, 256), BF16),
            pltpu.VMEM((3, 768, 384), BF16),
            pltpu.VMEM((32, 384), F32),
            pltpu.VMEM((128, 128), F32),
            pltpu.VMEM((768, 384), F32),
            pltpu.VMEM((768, 288), BF16),
            pltpu.VMEM((32, 384), F32),
            pltpu.VMEM((768, 512), F32),
            pltpu.VMEM((2, 768, 512), BF16),
            pltpu.VMEM((3, 768, 512), F32),
            pltpu.VMEM((768, 768), BF16),
            pltpu.VMEM((128, 128), F32),
            pltpu.SemaphoreType.DMA((11,)),
            pltpu.SemaphoreType.DMA((4,)),
        ],
        compiler_params=params,
        cost_estimate=pl.CostEstimate(flops=8 * 10**9, bytes_accessed=8 << 20, transcendentals=0),
        name="mid",
    )(
        levels.reshape(1, 128),
        owner,
        child,
        face_source.reshape(128, 6),
        by_field,
        tables["deriv_0"],
        tables["deriv_1"],
        tables["deriv_2"],
        table,
        large,
        tables["both"],
        flux_jac,
    )
    edge = tables["edge"]

    def post(*refs):
        post_kernel(*refs[:14], edge, *refs[14:])

    result = pl.pallas_call(
        post,
        out_shape=shape((768, 512)),
        in_specs=[HBM] * 12 + [SMEM] * 2,
        out_specs=HBM,
        scratch_shapes=[
            pltpu.VMEM((256, 128), F32),
            pltpu.VMEM((128, 512), F32),
            pltpu.VMEM((128, 384), F32),
            pltpu.VMEM((128, 384), F32),
            pltpu.VMEM((32, 384), F32),
            pltpu.VMEM((768, 288), BF16),
            pltpu.VMEM((768, 384), F32),
            pltpu.VMEM((256, 512), BF16),
            pltpu.VMEM((768, 512), F32),
            pltpu.VMEM((768, 384), F32),
            pltpu.VMEM((768, 128), F32),
            pltpu.VMEM((3, 768, 256), BF16),
            pltpu.VMEM((768, 512), F32),
            pltpu.SemaphoreType.DMA((12,)),
            pltpu.SemaphoreType.DMA((3,)),
        ],
        compiler_params=params,
        cost_estimate=pl.CostEstimate(flops=2 * 10**9, bytes_accessed=4 << 20, transcendentals=0),
        name="post",
    )(
        got.reshape(256, 128),
        tables["project"],
        *arrived,
        small,
        own_back,
        remote,
        local,
        tables["lift"],
        minus_volume,
        flux_jac,
        penalty,
    )
    return result.reshape(6, 128, 512).transpose(1, 0, 2)


def solution(mesh):
    in_specs = (
        P(("gx", "gy"), None, None),
        P(("gx", "gy")),
        P(("gx", "gy")),
        P(("gx", "gy"), None, None),
        P(("gx", "gy"), None, None),
        P(("gx", "gy"), None, None),
        P(),
        P(),
    )
    out_specs = P(("gx", "gy"), None, None)
    return jax.shard_map(
        per_device, mesh=mesh, in_specs=in_specs, out_specs=out_specs, check_vma=False
    )
```

```python
import jax
import jax.numpy as jnp
import ml_dtypes
import numpy as np
from jax import lax
from jax.experimental import pallas as pl
from jax.experimental.pallas import tpu as pltpu
from jax.sharding import PartitionSpec as P

P_SIZE = 7
OFFSETS = (-2, -1, 1, 2)
STEP_SIZE = 0.01

F32 = jnp.float32
BF16 = jnp.bfloat16
HIGHEST = lax.Precision.HIGHEST
VMEM = pl.BlockSpec(memory_space=pltpu.VMEM)
HBM = pl.BlockSpec(memory_space=pltpu.HBM)
MIB = 1 << 20


def shifted(value, axis, steps):
    count = lax.axis_size(axis)
    pairs = [(source, (source + steps) % count) for source in range(count)]
    return lax.ppermute(value, axis, pairs)


def pieces_of(table):
    rest = np.asarray(table, np.float32)
    out = []
    for _ in range(2):
        piece = rest.astype(ml_dtypes.bfloat16)
        out.append(piece)
        rest = rest - piece.astype(np.float32)
    return np.stack(out)


def basis_tables(order):
    per_dim = order + 1
    eye_small = np.eye(per_dim)
    points = -np.cos(np.pi * np.arange(per_dim) / order)
    differences = points[:, None] - points[None, :] + eye_small
    barycentric = 1.0 / np.prod(differences, axis=1)
    derivative = barycentric[None, :] / barycentric[:, None] / differences
    derivative = np.where(eye_small > 0, 0.0, derivative)
    derivative = derivative - eye_small * derivative.sum(axis=1)[:, None]
    angles = np.pi * np.arange(per_dim) / order
    weights = np.ones(per_dim)
    for wave in range(1, order // 2 + 1):
        factor = 1.0 if 2 * wave == order else 2.0
        weights = weights - factor * np.cos(2.0 * wave * angles) / (4.0 * wave * wave - 1.0)
    edge_factor = np.where((np.arange(per_dim) == 0) | (np.arange(per_dim) == order), 1.0, 2.0)
    weights = edge_factor * weights / order

    def lagrange(targets):
        values_at = np.ones((per_dim, per_dim))
        for column in range(per_dim):
            for other in range(per_dim):
                if other != column:
                    values_at[:, column] *= (targets - points[other]) / (
                        points[column] - points[other]
                    )
        return values_at

    halves = [lagrange((points - 1.0) / 2.0), lagrange((points + 1.0) / 2.0)]
    identity = np.eye(per_dim)
    node_index = np.arange(per_dim**3).reshape(per_dim, per_dim, per_dim)
    fnodes = per_dim * per_dim
    select = np.zeros((per_dim**3, 4 * fnodes), np.float32)
    for face in range(2, 6):
        picker = [slice(None), slice(None), slice(None)]
        picker[face // 2] = 0 if face % 2 == 0 else order
        on_face = node_index[tuple(picker)].reshape(-1)
        select[on_face, (face - 2) * fnodes + np.arange(fnodes)] = 1.0
    face_weight = np.kron(weights, weights)
    proj = [np.kron(halves[quad // 2], halves[quad % 2]) for quad in range(4)]
    restrict = [
        0.25 * (proj[quad].T * face_weight[None, :]) / face_weight[:, None] for quad in range(4)
    ]
    two = np.eye(2)
    both = sum(restrict[quad] @ proj[quad] for quad in range(4))
    quarter = np.eye(4)
    return {
        "select": select.astype(ml_dtypes.bfloat16),
        "lift": np.concatenate([select.T, select.T], 0).astype(ml_dtypes.bfloat16),
        "restrict": np.concatenate([np.kron(two, r.T) for r in restrict], 0).astype(np.float32),
        "project": np.concatenate([np.kron(two, p.T) for p in proj], 1).astype(np.float32),
        "both": np.kron(two, both.T).astype(np.float32),
        "deriv_0": pieces_of(np.kron(derivative, np.eye(fnodes)).T),
        "deriv_1": pieces_of(np.kron(quarter, np.kron(derivative, identity)).T),
        "deriv_2": pieces_of(np.kron(quarter, np.kron(identity, derivative)).T),
        "edge": float(1.0 / weights[0]),
    }


def split3(value):
    high = value.astype(BF16)
    rest = value - high.astype(F32)
    middle = rest.astype(BF16)
    low = (rest - middle.astype(F32)).astype(BF16)
    return high, middle, low


def mm(a, b):
    return jnp.dot(a, b, preferred_element_type=F32)


def low_half(rows):
    return lax.broadcasted_iota(jnp.int32, (rows, 128), 1) < 64


def swap_halves(value):
    return pltpu.roll(value, 64, 1)


def column_of(row):
    count = row.shape[1]
    spread = jnp.broadcast_to(row.astype(F32), (count, count))
    down = lax.broadcasted_iota(jnp.int32, (count, count), 0)
    across = lax.broadcasted_iota(jnp.int32, (count, count), 1)
    return jnp.sum(jnp.where(down == across, spread, 0.0), axis=1, keepdims=True).astype(jnp.int32)


def start_all(sources, targets, arrivals):
    copies = [
        pltpu.make_async_copy(source, target, arrivals.at[at])
        for at, (source, target) in enumerate(zip(sources, targets, strict=True))
    ]
    for copy in copies:
        copy.start()
    return copies


def rows_of(field):
    return slice(128 * field, 128 * field + 128)


def slot_or_spare(slot):
    return jnp.where(slot < 0, 768, slot)


def pre_kernel(
    state_far, send_far, owner_far, child_far, select_far, restrict_far,
    s0_far, s1_far, s2_far, s3_far, mort_far, table_far, large_far,
    state, send, owner, child, select, restrict, pieces, table, picked, mort, arrivals, sent,
):
    copies = start_all(
        [*(state_far.at[rows_of(f)] for f in range(6)), select_far, send_far, owner_far, child_far, restrict_far],
        [*(state.at[rows_of(f)] for f in range(6)), select, send, owner, child, restrict],
        arrivals,
    )
    low = low_half(128)
    table[:, 768:776] = jnp.zeros((3, 8, 128), F32)
    for part in (6, 7):
        mort[pl.ds(part, 32, stride=8), :] = jnp.zeros((32, 128), F32)
    for field in range(6):
        copies[field].wait()
        for piece, value in enumerate(split3(state[rows_of(field)])):
            pieces[piece, rows_of(field)] = value
    copies[6].wait()
    inner = (
        mm(pieces[0], select[...]) + mm(pieces[1], select[...]) + mm(pieces[2], select[...])
    )
    for pair in range(3):
        even, odd = rows_of(2 * pair), rows_of(2 * pair + 1)
        fronts = [(state[even, :128], state[odd, :128])]
        backs = [(state[even, 384:], state[odd, 384:])]
        for dim in range(2):
            at = slice(128 * dim, 128 * dim + 128)
            fronts.append((inner[even, at], inner[odd, at]))
        backs += fronts[1:]
        for dim in range(3):
            front = jnp.where(low, fronts[dim][0], swap_halves(fronts[dim][1]))
            back = jnp.where(low, swap_halves(backs[dim][0]), backs[dim][1])
            table[pair, pl.ds(2 * dim, 128, stride=6), :] = front
            table[pair, pl.ds(2 * dim + 1, 128, stride=6), :] = back
    leaving = start_all([table.at[:, 0:768]], [table_far], sent)
    for copy in copies[7:]:
        copy.wait()

    def move(out, row, slot):
        for pair in range(3):
            out[row : row + 1, 128 * pair : 128 * pair + 128] = table[pair, pl.ds(slot, 1), :]

    for q in range(4):
        for at in range(32):
            move(picked, 32 + 32 * q + at, slot_or_spare(child[q, at]))
    for at in range(32):
        move(picked, at, slot_or_spare(owner[0, at]))
    for o, out in enumerate((s0_far, s1_far, s2_far, s3_far)):
        for at in range(32):
            move(picked, 160 + 32 * o + at, send[o, at])
        leaving += start_all([picked.at[160 + 32 * o : 192 + 32 * o]], [out], sent.at[2 + o : 3 + o])
    leaving += start_all([picked.at[0:32]], [large_far], sent.at[1:2])
    for part in range(3):
        mort[pl.ds(3 + part, 32, stride=8), :] = picked[0:32, 128 * part : 128 * part + 128]
    stacked = jnp.concatenate(
        [
            jnp.concatenate(
                [
                    picked[32 + 32 * q : 64 + 32 * q, 128 * part : 128 * part + 128]
                    for q in range(4)
                ],
                1,
            )
            for part in range(3)
        ],
        0,
    )
    back = jnp.dot(stacked, restrict[...], precision=HIGHEST, preferred_element_type=F32)
    for part in range(3):
        mort[pl.ds(part, 32, stride=8), :] = back[32 * part : 32 * part + 32]
    leaving += start_all([mort], [mort_far], sent.at[6:7])
    for copy in leaving:
        copy.wait()


def wanted_column(sources, face):
    down = lax.broadcasted_iota(jnp.int32, (128, 128), 0)
    across = lax.broadcasted_iota(jnp.int32, (128, 128), 1)
    spread = jnp.zeros((128, 128), F32)
    for part in range(6):
        hit = across + 128 * part == 6 * down + face
        spread = jnp.where(hit, sources[part : part + 1], spread)
    return jnp.sum(spread, axis=1, keepdims=True).astype(jnp.int32)


def add_owned(jumps, owner, levels, rows, sign):
    for at in range(32):
        slot = owner[0, at]
        element = jnp.where(slot < 0, 0, (slot * 10923) >> 16)
        scale = sign * (1 << levels[0, element]).astype(F32)
        row = (slot - 6 * element) * 128 + element
        target = pl.ds(jnp.where(slot < 0, 768, row), 1)
        jumps[target] = jumps[target] + scale * rows[at : at + 1]


def by_field_order(jumps, values):
    low = low_half(128)
    for dim in range(3):
        at = slice(128 * dim, 128 * dim + 128)
        for pair in range(3):
            lanes = slice(128 * pair, 128 * pair + 128)
            front = jumps[256 * dim : 256 * dim + 128, lanes]
            back = jumps[256 * dim + 128 : 256 * dim + 256, lanes]
            values[rows_of(2 * pair), at] = jnp.where(low, front, swap_halves(back))
            values[rows_of(2 * pair + 1), at] = jnp.where(low, swap_halves(front), back)


def add_surface(values, flux, penalty, factor, surfaces, lift, out, out_far, ready, done):
    step = 32
    low = low_half(step)
    signs = jnp.where(low, -factor, factor)
    sent = []
    for pair in range(3):
        rows = slice(256 * pair, 256 * pair + 256)
        ready(pair)
        for field in (2 * pair, 2 * pair + 1):
            drag = factor * penalty[field]
            for dim in range(3):
                lanes = slice(128 * dim, 128 * dim + 128)
                rates = [flux[dim, field, other] for other in range(6)]
                for first in range(0, 128, step):
                    mixed = rates[0] * values[first : first + step, lanes]
                    for other in range(1, 6):
                        at = 128 * other + first
                        mixed = mixed + rates[other] * values[at : at + step, lanes]
                    at = 128 * field + first
                    surface = signs * mixed - drag * values[at : at + step, lanes]
                    if dim == 0:
                        out[at : at + step, 0:128] += jnp.where(low, surface, 0.0)
                        out[at : at + step, 384:512] += jnp.where(low, 0.0, surface)
                    else:
                        high = surface.astype(BF16)
                        surfaces[at : at + step, 128 * dim - 128 : 128 * dim] = high
                        rest = (surface - high.astype(F32)).astype(BF16)
                        surfaces[at : at + step, 128 * dim + 128 : 128 * dim + 256] = rest
        out[rows] += mm(surfaces[rows], lift[...])
        copy = pltpu.make_async_copy(out.at[rows], out_far.at[rows], done.at[pair])
        copy.start()
        sent.append(copy)
    return sent


def mid_kernel(
    levels_far, child_far, source_far, flux_far, penalty_far, owner_far, state_far, d0_far, d1_far,
    d2_far, table_far, large_far, both_far, lift_far, edge, out_far,
    levels, child, source, flux, penalty, owner, levels_near, state, d0, d1, d2, table, large, both,
    lift, out, pieces, grads, matrix, amount, traces, jumps, values, surfaces,
    arrivals, sent,
):
    copies = start_all(
        [levels_far, child_far, source_far], [levels, child, source], arrivals.at[0:3]
    )
    state_copies = start_all(
        [state_far.at[rows_of(f)] for f in range(6)],
        [state.at[rows_of(f)] for f in range(6)],
        arrivals.at[3:9],
    )
    copies += [None] + start_all(
        [flux_far, penalty_far, d0_far, d1_far, d2_far, owner_far, levels_far],
        [flux, penalty, d0, d1, d2, owner, levels_near],
        arrivals.at[9:16],
    )
    for copy in copies[:3]:
        copy.wait()
    level = column_of(levels[...])
    twos = (1 << level).astype(F32)
    minus = -twos
    amount[...] = jnp.broadcast_to(minus * STEP_SIZE, (128, 128))
    slots = lax.broadcasted_iota(jnp.int32, (1, 768), 1)
    element = lax.broadcasted_iota(jnp.int32, (128, 1), 0)
    child_row = jnp.concatenate([child[q : q + 1, :] for q in range(4)], 1)
    sources = source[...].astype(F32)
    for face in range(6):
        wanted = wanted_column(sources, face)
        mine = 6 * element + face
        rows = rows_of(face)
        as_child = jnp.where(mine == child_row, twos, 0.0)
        own = jnp.where(wanted >= 0, twos, 0.0) + jnp.sum(as_child, axis=1, keepdims=True)
        for other in range(6):
            at = slots[:, rows_of(other)]
            block = jnp.where(wanted == at, minus, 0.0) + jnp.where(mine == at, own, 0.0)
            matrix[rows, rows_of(other)] = block.astype(BF16)
    for field in range(6):
        state_copies[field].wait()
        rows = rows_of(field)
        value = state[rows]
        high = value.astype(BF16)
        pieces[0, rows] = high
        pieces[1, rows] = (value - high.astype(F32)).astype(BF16)
    later = start_all(
        [table_far, large_far, both_far, lift_far], [table, large, both, lift], arrivals.at[17:21]
    )
    for copy in copies[6:9]:
        copy.wait()

    def apply(lanes, deriv):
        high, rest = pieces[0, :, lanes], pieces[1, :, lanes]
        return mm(high, deriv[0]) + (mm(high, deriv[1]) + mm(rest, deriv[0]))

    grads[0] = apply(slice(0, 512), d0)
    for half in range(2):
        lanes = slice(256 * half, 256 * half + 256)
        grads[1, :, lanes] = apply(lanes, d1)
        grads[2, :, lanes] = apply(lanes, d2)
    for copy in later + copies[4:6]:
        copy.wait()
    for first in range(0, 128, 16):
        scale = amount[first : first + 16]
        scale = jnp.concatenate([scale] * 4, 1)
        for field in range(6):
            total = None
            for dim in range(3):
                for other in range(6):
                    rows = slice(128 * other + first, 128 * other + first + 16)
                    term = flux[dim, field, other] * grads[dim, rows, :]
                    total = term if total is None else total + term
            out[128 * field + first : 128 * field + first + 16] = scale * total
    for pair in range(3):
        for piece, value in enumerate(split3(table[pair])):
            first = 384 * piece + 128 * pair
            traces[:, first : first + 128] = value
    back = jnp.concatenate(
        [
            jnp.dot(
                large[:, 128 * part : 128 * part + 128],
                both[...],
                precision=HIGHEST,
                preferred_element_type=F32,
            )
            for part in range(3)
        ],
        1,
    )
    total = mm(matrix[...], traces[...])
    jumps[0:768] = total[:, 0:384] + total[:, 384:768] + total[:, 768:1152]
    copies[9].wait()
    copies[10].wait()
    add_owned(jumps, owner, levels_near, back, 1.0)
    by_field_order(jumps, values)
    leaving = add_surface(
        values, flux, penalty, 0.5 * STEP_SIZE * edge, surfaces, lift, out, out_far,
        lambda pair: None, sent,
    )
    for copy in leaving:
        copy.wait()


def post_kernel(
    got, a0, a1, a2, a3, project, source, child, levels_row, flux_far, penalty_far, owner_far,
    levels_far, lift_far, local_far, edge, out_far,
    flux, penalty, owner, levels, lift, out, remote, extra, jumps, values, surfaces,
    arrivals, done,
):
    thirds = [slice(256 * pair, 256 * pair + 256) for pair in range(3)]
    copies = start_all(
        [flux_far, penalty_far, owner_far, levels_far, lift_far, *(local_far.at[rows] for rows in thirds)],
        [flux, penalty, owner, levels, lift, *(out.at[rows] for rows in thirds)],
        arrivals,
    )
    minus = -(1 << column_of(levels_row[...])).astype(F32)
    element = lax.broadcasted_iota(jnp.int32, (128, 1), 0)
    arrived_slot = 768 + lax.broadcasted_iota(jnp.int32, (1, 128), 1)
    child_row = jnp.concatenate([child[q : q + 1, :] for q in range(4)], 1)
    sources = source[...].astype(F32)
    for face in range(6):
        wanted, mine = wanted_column(sources, face), 6 * element + face
        remote[rows_of(face), 0:128] = jnp.where(wanted == arrived_slot, minus, 0.0).astype(BF16)
        remote[rows_of(face), 128:256] = jnp.where(mine == child_row, minus, 0.0).astype(BF16)
    for place, rows in enumerate((a0, a1, a2, a3)):
        for piece, value in enumerate(split3(rows[...])):
            extra[32 * place : 32 * place + 32, 384 * piece : 384 * piece + 384] = value
    got_back = [got[pl.ds(part, 32, stride=8), :] for part in range(3)]
    got_large = [got[pl.ds(3 + part, 32, stride=8), :] for part in range(3)]
    onto = jnp.dot(
        jnp.concatenate(got_large, 0), project[...], precision=HIGHEST, preferred_element_type=F32
    )
    for piece, value in enumerate(split3(onto)):
        for part in range(3):
            lanes = slice(384 * piece + 128 * part, 384 * piece + 128 * part + 128)
            for q in range(4):
                extra[128 + 32 * q : 160 + 32 * q, lanes] = value[
                    32 * part : 32 * part + 32, 128 * q : 128 * q + 128
                ]
    total = mm(remote[...], extra[...])
    jumps[0:768] = total[:, 0:384] + total[:, 384:768] + total[:, 768:1152]
    for copy in copies[:5]:
        copy.wait()
    add_owned(jumps, owner, levels, jnp.concatenate(got_back, 1), -1.0)
    by_field_order(jumps, values)
    sent = add_surface(
        values, flux, penalty, 0.5 * STEP_SIZE * edge, surfaces, lift, out, out_far,
        lambda pair: copies[5 + pair].wait(), done,
    )
    for copy in sent:
        copy.wait()


def per_device(state, levels, face_source, face_send, mort_owner, mort_child, flux_jac, penalty):
    tables = basis_tables(P_SIZE)
    by_field = state.transpose(1, 0, 2).reshape(768, 512)
    send = face_send.reshape(4, 32)
    owner = mort_owner.reshape(1, 32)
    child = mort_child.transpose(0, 2, 1).reshape(4, 32)

    def shape(dims, kind=F32):
        return jax.ShapeDtypeStruct(dims, kind)

    def params(mib):
        return pltpu.CompilerParams(vmem_limit_bytes=mib * MIB)

    s0, s1, s2, s3, mort, table, large = pl.pallas_call(
        pre_kernel,
        out_shape=[shape((32, 384))] * 4
        + [shape((256, 128)), shape((3, 768, 128)), shape((32, 384))],
        in_specs=[HBM] * 6,
        out_specs=[HBM] * 7,
        scratch_shapes=[
            pltpu.VMEM((768, 512), F32),
            pltpu.SMEM((4, 32), jnp.int32),
            pltpu.SMEM((1, 32), jnp.int32),
            pltpu.SMEM((4, 32), jnp.int32),
            pltpu.VMEM((512, 256), BF16),
            pltpu.VMEM((512, 128), F32),
            pltpu.VMEM((3, 768, 512), BF16),
            pltpu.VMEM((3, 776, 128), F32),
            pltpu.VMEM((288, 384), F32),
            pltpu.VMEM((256, 128), F32),
            pltpu.SemaphoreType.DMA((11,)),
            pltpu.SemaphoreType.DMA((7,)),
        ],
        compiler_params=params(60),
        cost_estimate=pl.CostEstimate(flops=10**9, bytes_accessed=4 << 20, transcendentals=0),
        name="pre",
    )(by_field, send, owner, child, tables["select"], tables["restrict"])
    arrived = [
        shifted(rows, ("gx", "gy"), OFFSETS[place]) for place, rows in enumerate((s0, s1, s2, s3))
    ]
    got = lax.all_to_all(mort.reshape(32, 8, 128), "gy", split_axis=0, concat_axis=0, tiled=True)
    edge = tables["edge"]

    def mid(*refs):
        mid_kernel(*refs[:14], edge, *refs[14:])

    local = pl.pallas_call(
        mid,
        out_shape=shape((768, 512)),
        in_specs=[HBM] * 14,
        out_specs=HBM,
        scratch_shapes=[
            pltpu.VMEM((1, 128), jnp.int32),
            pltpu.VMEM((4, 32), jnp.int32),
            pltpu.VMEM((6, 128), jnp.int32),
            pltpu.SMEM((3, 6, 6), F32),
            pltpu.SMEM((6,), F32),
            pltpu.SMEM((1, 32), jnp.int32),
            pltpu.SMEM((1, 128), jnp.int32),
            pltpu.VMEM((768, 512), F32),
            pltpu.VMEM((2, 512, 512), BF16),
            pltpu.VMEM((2, 256, 256), BF16),
            pltpu.VMEM((2, 256, 256), BF16),
            pltpu.VMEM((3, 768, 128), F32),
            pltpu.VMEM((32, 384), F32),
            pltpu.VMEM((128, 128), F32),
            pltpu.VMEM((512, 512), BF16),
            pltpu.VMEM((768, 512), F32),
            pltpu.VMEM((2, 768, 512), BF16),
            pltpu.VMEM((3, 768, 512), F32),
            pltpu.VMEM((768, 768), BF16),
            pltpu.VMEM((128, 128), F32),
            pltpu.VMEM((768, 1152), BF16),
            pltpu.VMEM((776, 384), F32),
            pltpu.VMEM((768, 384), F32),
            pltpu.VMEM((768, 512), BF16),
            pltpu.SemaphoreType.DMA((21,)),
            pltpu.SemaphoreType.DMA((3,)),
        ],
        compiler_params=params(60),
        cost_estimate=pl.CostEstimate(flops=8 * 10**9, bytes_accessed=8 << 20, transcendentals=0),
        name="mid",
    )(
        levels.reshape(1, 128),
        child,
        face_source.reshape(6, 128),
        flux_jac,
        penalty,
        owner,
        by_field,
        tables["deriv_0"],
        tables["deriv_1"],
        tables["deriv_2"],
        table,
        large,
        tables["both"],
        tables["lift"],
    )

    def post(*refs):
        post_kernel(*refs[:15], edge, *refs[15:])

    result = pl.pallas_call(
        post,
        out_shape=shape((768, 512)),
        in_specs=[VMEM] * 9 + [HBM] * 6,
        out_specs=HBM,
        input_output_aliases={14: 0},
        scratch_shapes=[
            pltpu.SMEM((3, 6, 6), F32),
            pltpu.SMEM((6,), F32),
            pltpu.SMEM((1, 32), jnp.int32),
            pltpu.SMEM((1, 128), jnp.int32),
            pltpu.VMEM((512, 512), BF16),
            pltpu.VMEM((768, 512), F32),
            pltpu.VMEM((768, 256), BF16),
            pltpu.VMEM((256, 1152), BF16),
            pltpu.VMEM((776, 384), F32),
            pltpu.VMEM((768, 384), F32),
            pltpu.VMEM((768, 512), BF16),
            pltpu.SemaphoreType.DMA((8,)),
            pltpu.SemaphoreType.DMA((3,)),
        ],
        compiler_params=params(32),
        cost_estimate=pl.CostEstimate(flops=2 * 10**9, bytes_accessed=4 << 20, transcendentals=0),
        name="post",
    )(
        got.reshape(256, 128),
        *arrived,
        tables["project"],
        face_source.reshape(6, 128),
        child,
        levels.reshape(1, 128),
        flux_jac,
        penalty,
        owner,
        levels.reshape(1, 128),
        tables["lift"],
        local,
    )
    return result.reshape(6, 128, 512).transpose(1, 0, 2)


def solution(mesh):
    in_specs = (
        P(("gx", "gy"), None, None),
        P(("gx", "gy")),
        P(("gx", "gy")),
        P(("gx", "gy"), None, None),
        P(("gx", "gy"), None, None),
        P(("gx", "gy"), None, None),
        P(),
        P(),
    )
    out_specs = P(("gx", "gy"), None, None)
    return jax.shard_map(
        per_device, mesh=mesh, in_specs=in_specs, out_specs=out_specs, check_vma=False
    )
```

```python
import jax
import jax.numpy as jnp
import ml_dtypes
import numpy as np
from jax import lax
from jax.experimental import pallas as pl
from jax.experimental.pallas import tpu as pltpu
from jax.sharding import PartitionSpec as P

P_SIZE = 7
OFFSETS = (-2, -1, 1, 2)
STEP_SIZE = 0.01

F32 = jnp.float32
BF16 = jnp.bfloat16
HIGHEST = lax.Precision.HIGHEST
VMEM = pl.BlockSpec(memory_space=pltpu.VMEM)
HBM = pl.BlockSpec(memory_space=pltpu.HBM)
MIB = 1 << 20


def shifted(value, axis, steps):
    count = lax.axis_size(axis)
    pairs = [(source, (source + steps) % count) for source in range(count)]
    return lax.ppermute(value, axis, pairs)


def pieces_of(table):
    rest = np.asarray(table, np.float32)
    out = []
    for _ in range(2):
        piece = rest.astype(ml_dtypes.bfloat16)
        out.append(piece)
        rest = rest - piece.astype(np.float32)
    return np.stack(out)


def basis_tables(order):
    per_dim = order + 1
    eye_small = np.eye(per_dim)
    points = -np.cos(np.pi * np.arange(per_dim) / order)
    differences = points[:, None] - points[None, :] + eye_small
    barycentric = 1.0 / np.prod(differences, axis=1)
    derivative = barycentric[None, :] / barycentric[:, None] / differences
    derivative = np.where(eye_small > 0, 0.0, derivative)
    derivative = derivative - eye_small * derivative.sum(axis=1)[:, None]
    angles = np.pi * np.arange(per_dim) / order
    weights = np.ones(per_dim)
    for wave in range(1, order // 2 + 1):
        factor = 1.0 if 2 * wave == order else 2.0
        weights = weights - factor * np.cos(2.0 * wave * angles) / (4.0 * wave * wave - 1.0)
    edge_factor = np.where((np.arange(per_dim) == 0) | (np.arange(per_dim) == order), 1.0, 2.0)
    weights = edge_factor * weights / order

    def lagrange(targets):
        values_at = np.ones((per_dim, per_dim))
        for column in range(per_dim):
            for other in range(per_dim):
                if other != column:
                    values_at[:, column] *= (targets - points[other]) / (
                        points[column] - points[other]
                    )
        return values_at

    halves = [lagrange((points - 1.0) / 2.0), lagrange((points + 1.0) / 2.0)]
    identity = np.eye(per_dim)
    node_index = np.arange(per_dim**3).reshape(per_dim, per_dim, per_dim)
    fnodes = per_dim * per_dim
    select = np.zeros((per_dim**3, 4 * fnodes), np.float32)
    for face in range(2, 6):
        picker = [slice(None), slice(None), slice(None)]
        picker[face // 2] = 0 if face % 2 == 0 else order
        on_face = node_index[tuple(picker)].reshape(-1)
        select[on_face, (face - 2) * fnodes + np.arange(fnodes)] = 1.0
    face_weight = np.kron(weights, weights)
    proj = [np.kron(halves[quad // 2], halves[quad % 2]) for quad in range(4)]
    restrict = [
        0.25 * (proj[quad].T * face_weight[None, :]) / face_weight[:, None] for quad in range(4)
    ]
    two = np.eye(2)
    both = sum(restrict[quad] @ proj[quad] for quad in range(4))
    quarter = np.eye(4)
    return {
        "select": select.astype(ml_dtypes.bfloat16),
        "lift": np.concatenate([select.T, select.T], 0).astype(ml_dtypes.bfloat16),
        "restrict": np.concatenate([np.kron(two, r.T) for r in restrict], 0).astype(np.float32),
        "project": np.concatenate([np.kron(two, p.T) for p in proj], 1).astype(np.float32),
        "both": np.kron(two, both.T).astype(np.float32),
        "deriv_0": pieces_of(np.kron(derivative, np.eye(fnodes)).T),
        "deriv_1": pieces_of(np.kron(quarter, np.kron(derivative, identity)).T),
        "deriv_2": pieces_of(np.kron(quarter, np.kron(identity, derivative)).T),
        "edge": float(1.0 / weights[0]),
    }


def split3(value):
    high = value.astype(BF16)
    rest = value - high.astype(F32)
    middle = rest.astype(BF16)
    low = (rest - middle.astype(F32)).astype(BF16)
    return high, middle, low


def mm(a, b):
    return jnp.dot(a, b, preferred_element_type=F32)


def low_half(rows):
    return lax.broadcasted_iota(jnp.int32, (rows, 128), 1) < 64


def swap_halves(value):
    return pltpu.roll(value, 64, 1)


def column_of(row):
    count = row.shape[1]
    spread = jnp.broadcast_to(row.astype(F32), (count, count))
    down = lax.broadcasted_iota(jnp.int32, (count, count), 0)
    across = lax.broadcasted_iota(jnp.int32, (count, count), 1)
    return jnp.sum(jnp.where(down == across, spread, 0.0), axis=1, keepdims=True).astype(jnp.int32)


def start_all(sources, targets, arrivals):
    copies = [
        pltpu.make_async_copy(source, target, arrivals.at[at])
        for at, (source, target) in enumerate(zip(sources, targets, strict=True))
    ]
    for copy in copies:
        copy.start()
    return copies


def rows_of(field):
    return slice(128 * field, 128 * field + 128)


def slot_or_spare(slot):
    return jnp.where(slot < 0, 768, slot)


def pre_kernel(
    state_far, send_far, owner_far, child_far, select_far, restrict_far,
    s0_far, s1_far, s2_far, s3_far, mort_far, table_far, large_far,
    state, send, owner, child, select, restrict, pieces, table, picked, mort, arrivals, sent,
):
    copies = start_all(
        [*(state_far.at[rows_of(f)] for f in range(6)), select_far, send_far, owner_far, child_far, restrict_far],
        [*(state.at[rows_of(f)] for f in range(6)), select, send, owner, child, restrict],
        arrivals,
    )
    low = low_half(128)
    table[:, 768:776] = jnp.zeros((3, 8, 128), F32)
    for part in (6, 7):
        mort[pl.ds(part, 32, stride=8), :] = jnp.zeros((32, 128), F32)
    for field in range(6):
        copies[field].wait()
        for piece, value in enumerate(split3(state[rows_of(field)])):
            pieces[piece, rows_of(field)] = value
    copies[6].wait()
    inner = (
        mm(pieces[0], select[...]) + mm(pieces[1], select[...]) + mm(pieces[2], select[...])
    )
    for pair in range(3):
        even, odd = rows_of(2 * pair), rows_of(2 * pair + 1)
        fronts = [(state[even, :128], state[odd, :128])]
        backs = [(state[even, 384:], state[odd, 384:])]
        for dim in range(2):
            at = slice(128 * dim, 128 * dim + 128)
            fronts.append((inner[even, at], inner[odd, at]))
        backs += fronts[1:]
        for dim in range(3):
            front = jnp.where(low, fronts[dim][0], swap_halves(fronts[dim][1]))
            back = jnp.where(low, swap_halves(backs[dim][0]), backs[dim][1])
            table[pair, pl.ds(2 * dim, 128, stride=6), :] = front
            table[pair, pl.ds(2 * dim + 1, 128, stride=6), :] = back
    leaving = start_all([table.at[:, 0:768]], [table_far], sent)
    for copy in copies[7:]:
        copy.wait()

    def move(out, row, slot):
        for pair in range(3):
            out[row : row + 1, 128 * pair : 128 * pair + 128] = table[pair, pl.ds(slot, 1), :]

    for q in range(4):
        for at in range(32):
            move(picked, 32 + 32 * q + at, slot_or_spare(child[q, at]))
    for at in range(32):
        move(picked, at, slot_or_spare(owner[0, at]))
    for o, out in enumerate((s0_far, s1_far, s2_far, s3_far)):
        for at in range(32):
            move(picked, 160 + 32 * o + at, send[o, at])
        leaving += start_all([picked.at[160 + 32 * o : 192 + 32 * o]], [out], sent.at[2 + o : 3 + o])
    leaving += start_all([picked.at[0:32]], [large_far], sent.at[1:2])
    for part in range(3):
        mort[pl.ds(3 + part, 32, stride=8), :] = picked[0:32, 128 * part : 128 * part + 128]
    stacked = jnp.concatenate(
        [
            jnp.concatenate(
                [
                    picked[32 + 32 * q : 64 + 32 * q, 128 * part : 128 * part + 128]
                    for q in range(4)
                ],
                1,
            )
            for part in range(3)
        ],
        0,
    )
    back = jnp.dot(stacked, restrict[...], precision=HIGHEST, preferred_element_type=F32)
    for part in range(3):
        mort[pl.ds(part, 32, stride=8), :] = back[32 * part : 32 * part + 32]
    leaving += start_all([mort], [mort_far], sent.at[6:7])
    for copy in leaving:
        copy.wait()


def wanted_column(sources, face):
    down = lax.broadcasted_iota(jnp.int32, (128, 128), 0)
    across = lax.broadcasted_iota(jnp.int32, (128, 128), 1)
    spread = jnp.zeros((128, 128), F32)
    for part in range(6):
        hit = across + 128 * part == 6 * down + face
        spread = jnp.where(hit, sources[part : part + 1], spread)
    return jnp.sum(spread, axis=1, keepdims=True).astype(jnp.int32)


def add_owned(jumps, owner, levels, rows, sign):
    for at in range(32):
        slot = owner[0, at]
        element = jnp.where(slot < 0, 0, (slot * 10923) >> 16)
        scale = sign * (1 << levels[0, element]).astype(F32)
        row = (slot - 6 * element) * 128 + element
        target = pl.ds(jnp.where(slot < 0, 768, row), 1)
        jumps[target] = jumps[target] + scale * rows[at : at + 1]


def by_field_order(jumps, values, dim):
    low = low_half(128)
    at = slice(128 * dim, 128 * dim + 128)
    for pair in range(3):
        lanes = slice(128 * pair, 128 * pair + 128)
        front = jumps[256 * dim : 256 * dim + 128, lanes]
        back = jumps[256 * dim + 128 : 256 * dim + 256, lanes]
        values[rows_of(2 * pair), at] = jnp.where(low, front, swap_halves(back))
        values[rows_of(2 * pair + 1), at] = jnp.where(low, swap_halves(front), back)


def add_surface(values, flux, penalty, factor, surfaces, lift, out, out_far, ready, done):
    step = 32
    low = low_half(step)
    signs = jnp.where(low, -factor, factor)
    sent = []
    for pair in range(3):
        rows = slice(256 * pair, 256 * pair + 256)
        ready(pair)
        for field in (2 * pair, 2 * pair + 1):
            drag = factor * penalty[field]
            for dim in range(3):
                lanes = slice(128 * dim, 128 * dim + 128)
                rates = [flux[dim, field, other] for other in range(6)]
                for first in range(0, 128, step):
                    mixed = rates[0] * values[first : first + step, lanes]
                    for other in range(1, 6):
                        at = 128 * other + first
                        mixed = mixed + rates[other] * values[at : at + step, lanes]
                    at = 128 * field + first
                    surface = signs * mixed - drag * values[at : at + step, lanes]
                    if dim == 0:
                        out[at : at + step, 0:128] += jnp.where(low, surface, 0.0)
                        out[at : at + step, 384:512] += jnp.where(low, 0.0, surface)
                    else:
                        high = surface.astype(BF16)
                        surfaces[at : at + step, 128 * dim - 128 : 128 * dim] = high
                        rest = (surface - high.astype(F32)).astype(BF16)
                        surfaces[at : at + step, 128 * dim + 128 : 128 * dim + 256] = rest
        out[rows] += mm(surfaces[rows], lift[...])
        copy = pltpu.make_async_copy(out.at[rows], out_far.at[rows], done.at[pair])
        copy.start()
        sent.append(copy)
    return sent


def mid_kernel(
    levels_far, child_far, source_far, flux_far, penalty_far, owner_far, state_far, d0_far, d1_far,
    d2_far, table_far, large_far, both_far, lift_far, edge, out_far,
    levels, child, source, flux, penalty, owner, levels_near, state, d0, d1, d2, table, large, both,
    lift, out, pieces, grads, matrix, amount, traces, jumps, values, surfaces,
    arrivals, sent,
):
    copies = start_all(
        [levels_far, child_far, source_far], [levels, child, source], arrivals.at[0:3]
    )
    state_copies = start_all(
        [state_far.at[rows_of(f)] for f in range(6)],
        [state.at[rows_of(f)] for f in range(6)],
        arrivals.at[3:9],
    )
    copies += [None] + start_all(
        [flux_far, penalty_far, d0_far, d1_far, d2_far, owner_far, levels_far],
        [flux, penalty, d0, d1, d2, owner, levels_near],
        arrivals.at[9:16],
    )
    later = start_all(
        [table_far, large_far, both_far, lift_far], [table, large, both, lift], arrivals.at[17:21]
    )
    for copy in copies[:3]:
        copy.wait()
    level = column_of(levels[...])
    twos = (1 << level).astype(F32)
    minus = -twos
    amount[...] = jnp.broadcast_to(minus * STEP_SIZE, (128, 128))
    slots = lax.broadcasted_iota(jnp.int32, (1, 768), 1)
    element = lax.broadcasted_iota(jnp.int32, (128, 1), 0)
    child_row = jnp.concatenate([child[q : q + 1, :] for q in range(4)], 1)
    sources = source[...].astype(F32)
    for face in range(6):
        wanted = wanted_column(sources, face)
        mine = 6 * element + face
        rows = rows_of(face)
        as_child = jnp.where(mine == child_row, twos, 0.0)
        own = jnp.where(wanted >= 0, twos, 0.0) + jnp.sum(as_child, axis=1, keepdims=True)
        for other in range(6):
            at = slots[:, rows_of(other)]
            block = jnp.where(wanted == at, minus, 0.0) + jnp.where(mine == at, own, 0.0)
            matrix[rows, rows_of(other)] = block.astype(BF16)
    for field in range(6):
        state_copies[field].wait()
        rows = rows_of(field)
        value = state[rows]
        high = value.astype(BF16)
        pieces[0, rows] = high
        pieces[1, rows] = (value - high.astype(F32)).astype(BF16)
    for copy in later + copies[4:11]:
        copy.wait()

    def apply(lanes, deriv):
        high, rest = pieces[0, :, lanes], pieces[1, :, lanes]
        return mm(high, deriv[0]) + (mm(high, deriv[1]) + mm(rest, deriv[0]))

    grads[0] = apply(slice(0, 512), d0)
    for half in range(2):
        lanes = slice(256 * half, 256 * half + 256)
        grads[1, :, lanes] = apply(lanes, d1)
        grads[2, :, lanes] = apply(lanes, d2)
    for pair in range(3):
        for piece, value in enumerate(split3(table[pair])):
            first = 384 * piece + 128 * pair
            traces[:, first : first + 128] = value
    back = jnp.concatenate(
        [
            jnp.dot(
                large[:, 128 * part : 128 * part + 128],
                both[...],
                precision=HIGHEST,
                preferred_element_type=F32,
            )
            for part in range(3)
        ],
        1,
    )
    jumps[...] = jnp.zeros((776, 384), F32)
    add_owned(jumps, owner, levels_near, back, 1.0)

    def mix(first):
        scale = amount[first : first + 16]
        scale = jnp.concatenate([scale] * 4, 1)
        for field in range(6):
            total = None
            for dim in range(3):
                for other in range(6):
                    rows = slice(128 * other + first, 128 * other + first + 16)
                    term = flux[dim, field, other] * grads[dim, rows, :]
                    total = term if total is None else total + term
            out[128 * field + first : 128 * field + first + 16] = scale * total

    for dim in range(3):
        rows = slice(256 * dim, 256 * dim + 256)
        total = mm(matrix[rows], traces[...])
        for first in range(48 * dim, min(48 * dim + 48, 128), 16):
            mix(first)
        jumps[rows] += total[:, 0:384] + total[:, 384:768] + total[:, 768:1152]
        by_field_order(jumps, values, dim)
    leaving = add_surface(
        values, flux, penalty, 0.5 * STEP_SIZE * edge, surfaces, lift, out, out_far,
        lambda pair: None, sent,
    )
    for copy in leaving:
        copy.wait()


def post_kernel(
    got, a0, a1, a2, a3, project, source, child, levels_row, flux_far, penalty_far, owner_far,
    levels_far, lift_far, local_far, edge, out_far,
    flux, penalty, owner, levels, lift, out, remote, extra, jumps, values, surfaces,
    arrivals, done,
):
    thirds = [slice(256 * pair, 256 * pair + 256) for pair in range(3)]
    copies = start_all(
        [flux_far, penalty_far, owner_far, levels_far, lift_far, *(local_far.at[rows] for rows in thirds)],
        [flux, penalty, owner, levels, lift, *(out.at[rows] for rows in thirds)],
        arrivals,
    )
    minus = -(1 << column_of(levels_row[...])).astype(F32)
    element = lax.broadcasted_iota(jnp.int32, (128, 1), 0)
    arrived_slot = 768 + lax.broadcasted_iota(jnp.int32, (1, 128), 1)
    child_row = jnp.concatenate([child[q : q + 1, :] for q in range(4)], 1)
    sources = source[...].astype(F32)
    for face in range(6):
        wanted, mine = wanted_column(sources, face), 6 * element + face
        remote[rows_of(face), 0:128] = jnp.where(wanted == arrived_slot, minus, 0.0).astype(BF16)
        remote[rows_of(face), 128:256] = jnp.where(mine == child_row, minus, 0.0).astype(BF16)
    for place, rows in enumerate((a0, a1, a2, a3)):
        for piece, value in enumerate(split3(rows[...])):
            extra[32 * place : 32 * place + 32, 384 * piece : 384 * piece + 384] = value
    got_back = [got[pl.ds(part, 32, stride=8), :] for part in range(3)]
    got_large = [got[pl.ds(3 + part, 32, stride=8), :] for part in range(3)]
    onto = jnp.dot(
        jnp.concatenate(got_large, 0), project[...], precision=HIGHEST, preferred_element_type=F32
    )
    for piece, value in enumerate(split3(onto)):
        for part in range(3):
            lanes = slice(384 * piece + 128 * part, 384 * piece + 128 * part + 128)
            for q in range(4):
                extra[128 + 32 * q : 160 + 32 * q, lanes] = value[
                    32 * part : 32 * part + 32, 128 * q : 128 * q + 128
                ]
    for copy in copies[:5]:
        copy.wait()
    jumps[...] = jnp.zeros((776, 384), F32)
    add_owned(jumps, owner, levels, jnp.concatenate(got_back, 1), -1.0)
    for dim in range(3):
        rows = slice(256 * dim, 256 * dim + 256)
        total = mm(remote[rows], extra[...])
        jumps[rows] += total[:, 0:384] + total[:, 384:768] + total[:, 768:1152]
        by_field_order(jumps, values, dim)
    sent = add_surface(
        values, flux, penalty, 0.5 * STEP_SIZE * edge, surfaces, lift, out, out_far,
        lambda pair: copies[5 + pair].wait(), done,
    )
    for copy in sent:
        copy.wait()


def per_device(state, levels, face_source, face_send, mort_owner, mort_child, flux_jac, penalty):
    tables = basis_tables(P_SIZE)
    by_field = state.transpose(1, 0, 2).reshape(768, 512)
    send = face_send.reshape(4, 32)
    owner = mort_owner.reshape(1, 32)
    child = mort_child.transpose(0, 2, 1).reshape(4, 32)

    def shape(dims, kind=F32):
        return jax.ShapeDtypeStruct(dims, kind)

    def params(mib):
        return pltpu.CompilerParams(vmem_limit_bytes=mib * MIB)

    s0, s1, s2, s3, mort, table, large = pl.pallas_call(
        pre_kernel,
        out_shape=[shape((32, 384))] * 4
        + [shape((256, 128)), shape((3, 768, 128)), shape((32, 384))],
        in_specs=[HBM] * 6,
        out_specs=[HBM] * 7,
        scratch_shapes=[
            pltpu.VMEM((768, 512), F32),
            pltpu.SMEM((4, 32), jnp.int32),
            pltpu.SMEM((1, 32), jnp.int32),
            pltpu.SMEM((4, 32), jnp.int32),
            pltpu.VMEM((512, 256), BF16),
            pltpu.VMEM((512, 128), F32),
            pltpu.VMEM((3, 768, 512), BF16),
            pltpu.VMEM((3, 776, 128), F32),
            pltpu.VMEM((288, 384), F32),
            pltpu.VMEM((256, 128), F32),
            pltpu.SemaphoreType.DMA((11,)),
            pltpu.SemaphoreType.DMA((7,)),
        ],
        compiler_params=params(60),
        cost_estimate=pl.CostEstimate(flops=10**9, bytes_accessed=4 << 20, transcendentals=0),
        name="pre",
    )(by_field, send, owner, child, tables["select"], tables["restrict"])
    arrived = [
        shifted(rows, ("gx", "gy"), OFFSETS[place]) for place, rows in enumerate((s0, s1, s2, s3))
    ]
    got = lax.all_to_all(mort.reshape(32, 8, 128), "gy", split_axis=0, concat_axis=0, tiled=True)
    edge = tables["edge"]

    def mid(*refs):
        mid_kernel(*refs[:14], edge, *refs[14:])

    local = pl.pallas_call(
        mid,
        out_shape=shape((768, 512)),
        in_specs=[HBM] * 14,
        out_specs=HBM,
        scratch_shapes=[
            pltpu.VMEM((1, 128), jnp.int32),
            pltpu.VMEM((4, 32), jnp.int32),
            pltpu.VMEM((6, 128), jnp.int32),
            pltpu.SMEM((3, 6, 6), F32),
            pltpu.SMEM((6,), F32),
            pltpu.SMEM((1, 32), jnp.int32),
            pltpu.SMEM((1, 128), jnp.int32),
            pltpu.VMEM((768, 512), F32),
            pltpu.VMEM((2, 512, 512), BF16),
            pltpu.VMEM((2, 256, 256), BF16),
            pltpu.VMEM((2, 256, 256), BF16),
            pltpu.VMEM((3, 768, 128), F32),
            pltpu.VMEM((32, 384), F32),
            pltpu.VMEM((128, 128), F32),
            pltpu.VMEM((512, 512), BF16),
            pltpu.VMEM((768, 512), F32),
            pltpu.VMEM((2, 768, 512), BF16),
            pltpu.VMEM((3, 768, 512), F32),
            pltpu.VMEM((768, 768), BF16),
            pltpu.VMEM((128, 128), F32),
            pltpu.VMEM((768, 1152), BF16),
            pltpu.VMEM((776, 384), F32),
            pltpu.VMEM((768, 384), F32),
            pltpu.VMEM((768, 512), BF16),
            pltpu.SemaphoreType.DMA((21,)),
            pltpu.SemaphoreType.DMA((3,)),
        ],
        compiler_params=params(60),
        cost_estimate=pl.CostEstimate(flops=8 * 10**9, bytes_accessed=8 << 20, transcendentals=0),
        name="mid",
    )(
        levels.reshape(1, 128),
        child,
        face_source.reshape(6, 128),
        flux_jac,
        penalty,
        owner,
        by_field,
        tables["deriv_0"],
        tables["deriv_1"],
        tables["deriv_2"],
        table,
        large,
        tables["both"],
        tables["lift"],
    )

    def post(*refs):
        post_kernel(*refs[:15], edge, *refs[15:])

    result = pl.pallas_call(
        post,
        out_shape=shape((768, 512)),
        in_specs=[VMEM] * 9 + [HBM] * 6,
        out_specs=HBM,
        input_output_aliases={14: 0},
        scratch_shapes=[
            pltpu.SMEM((3, 6, 6), F32),
            pltpu.SMEM((6,), F32),
            pltpu.SMEM((1, 32), jnp.int32),
            pltpu.SMEM((1, 128), jnp.int32),
            pltpu.VMEM((512, 512), BF16),
            pltpu.VMEM((768, 512), F32),
            pltpu.VMEM((768, 256), BF16),
            pltpu.VMEM((256, 1152), BF16),
            pltpu.VMEM((776, 384), F32),
            pltpu.VMEM((768, 384), F32),
            pltpu.VMEM((768, 512), BF16),
            pltpu.SemaphoreType.DMA((8,)),
            pltpu.SemaphoreType.DMA((3,)),
        ],
        compiler_params=params(32),
        cost_estimate=pl.CostEstimate(flops=2 * 10**9, bytes_accessed=4 << 20, transcendentals=0),
        name="post",
    )(
        got.reshape(256, 128),
        *arrived,
        tables["project"],
        face_source.reshape(6, 128),
        child,
        levels.reshape(1, 128),
        flux_jac,
        penalty,
        owner,
        levels.reshape(1, 128),
        tables["lift"],
        local,
    )
    return result.reshape(6, 128, 512).transpose(1, 0, 2)


def solution(mesh):
    in_specs = (
        P(("gx", "gy"), None, None),
        P(("gx", "gy")),
        P(("gx", "gy")),
        P(("gx", "gy"), None, None),
        P(("gx", "gy"), None, None),
        P(("gx", "gy"), None, None),
        P(),
        P(),
    )
    out_specs = P(("gx", "gy"), None, None)
    return jax.shard_map(
        per_device, mesh=mesh, in_specs=in_specs, out_specs=out_specs, check_vma=False
    )
```

```python
import jax
import jax.numpy as jnp
import ml_dtypes
import numpy as np
from jax import lax
from jax.experimental import pallas as pl
from jax.experimental.pallas import tpu as pltpu
from jax.sharding import PartitionSpec as P

P_SIZE = 7
OFFSETS = (-2, -1, 1, 2)
STEP_SIZE = 0.01

F32 = jnp.float32
BF16 = jnp.bfloat16
HIGHEST = lax.Precision.HIGHEST
VMEM = pl.BlockSpec(memory_space=pltpu.VMEM)
HBM = pl.BlockSpec(memory_space=pltpu.HBM)
MIB = 1 << 20


def shifted(value, axis, steps):
    count = lax.axis_size(axis)
    pairs = [(source, (source + steps) % count) for source in range(count)]
    return lax.ppermute(value, axis, pairs)


def pieces_of(table):
    rest = np.asarray(table, np.float32)
    out = []
    for _ in range(2):
        piece = rest.astype(ml_dtypes.bfloat16)
        out.append(piece)
        rest = rest - piece.astype(np.float32)
    return np.stack(out)


def basis_tables(order):
    per_dim = order + 1
    eye_small = np.eye(per_dim)
    points = -np.cos(np.pi * np.arange(per_dim) / order)
    differences = points[:, None] - points[None, :] + eye_small
    barycentric = 1.0 / np.prod(differences, axis=1)
    derivative = barycentric[None, :] / barycentric[:, None] / differences
    derivative = np.where(eye_small > 0, 0.0, derivative)
    derivative = derivative - eye_small * derivative.sum(axis=1)[:, None]
    angles = np.pi * np.arange(per_dim) / order
    weights = np.ones(per_dim)
    for wave in range(1, order // 2 + 1):
        factor = 1.0 if 2 * wave == order else 2.0
        weights = weights - factor * np.cos(2.0 * wave * angles) / (4.0 * wave * wave - 1.0)
    edge_factor = np.where((np.arange(per_dim) == 0) | (np.arange(per_dim) == order), 1.0, 2.0)
    weights = edge_factor * weights / order

    def lagrange(targets):
        values_at = np.ones((per_dim, per_dim))
        for column in range(per_dim):
            for other in range(per_dim):
                if other != column:
                    values_at[:, column] *= (targets - points[other]) / (
                        points[column] - points[other]
                    )
        return values_at

    halves = [lagrange((points - 1.0) / 2.0), lagrange((points + 1.0) / 2.0)]
    identity = np.eye(per_dim)
    node_index = np.arange(per_dim**3).reshape(per_dim, per_dim, per_dim)
    fnodes = per_dim * per_dim
    select = np.zeros((per_dim**3, 4 * fnodes), np.float32)
    for face in range(2, 6):
        picker = [slice(None), slice(None), slice(None)]
        picker[face // 2] = 0 if face % 2 == 0 else order
        on_face = node_index[tuple(picker)].reshape(-1)
        select[on_face, (face - 2) * fnodes + np.arange(fnodes)] = 1.0
    face_weight = np.kron(weights, weights)
    proj = [np.kron(halves[quad // 2], halves[quad % 2]) for quad in range(4)]
    restrict = [
        0.25 * (proj[quad].T * face_weight[None, :]) / face_weight[:, None] for quad in range(4)
    ]
    two = np.eye(2)
    both = sum(restrict[quad] @ proj[quad] for quad in range(4))
    quarter = np.eye(4)
    return {
        "select": select.astype(ml_dtypes.bfloat16),
        "lift": np.concatenate([select.T, select.T], 0).astype(ml_dtypes.bfloat16),
        "restrict": np.concatenate([np.kron(two, r.T) for r in restrict], 0).astype(np.float32),
        "project": np.concatenate([np.kron(two, p.T) for p in proj], 1).astype(np.float32),
        "both": np.kron(two, both.T).astype(np.float32),
        "deriv_0": pieces_of(np.kron(derivative, np.eye(fnodes)).T),
        "deriv_1": pieces_of(np.kron(quarter, np.kron(derivative, identity)).T),
        "deriv_2": pieces_of(np.kron(quarter, np.kron(identity, derivative)).T),
        "edge": float(1.0 / weights[0]),
    }


def split3(value):
    high = value.astype(BF16)
    rest = value - high.astype(F32)
    middle = rest.astype(BF16)
    low = (rest - middle.astype(F32)).astype(BF16)
    return high, middle, low


def mm(a, b):
    return jnp.dot(a, b, preferred_element_type=F32)


def low_half(rows):
    return lax.broadcasted_iota(jnp.int32, (rows, 128), 1) < 64


def swap_halves(value):
    return pltpu.roll(value, 64, 1)


def column_of(row):
    count = row.shape[1]
    spread = jnp.broadcast_to(row.astype(F32), (count, count))
    down = lax.broadcasted_iota(jnp.int32, (count, count), 0)
    across = lax.broadcasted_iota(jnp.int32, (count, count), 1)
    return jnp.sum(jnp.where(down == across, spread, 0.0), axis=1, keepdims=True).astype(jnp.int32)


def start_all(sources, targets, arrivals):
    copies = [
        pltpu.make_async_copy(source, target, arrivals.at[at])
        for at, (source, target) in enumerate(zip(sources, targets, strict=True))
    ]
    for copy in copies:
        copy.start()
    return copies


def rows_of(field):
    return slice(128 * field, 128 * field + 128)


def slot_or_spare(slot):
    return jnp.where(slot < 0, 768, slot)


def pre_kernel(
    state_far, send_far, owner_far, child_far, select_far, restrict_far,
    s0_far, s1_far, s2_far, s3_far, mort_far, table_far, large_far,
    state, send, owner, child, select, restrict, pieces, table, picked, mort, arrivals, sent,
):
    copies = start_all(
        [*(state_far.at[rows_of(f)] for f in range(6)), select_far, send_far, owner_far, child_far, restrict_far],
        [*(state.at[rows_of(f)] for f in range(6)), select, send, owner, child, restrict],
        arrivals,
    )
    low = low_half(128)
    table[:, 768:776] = jnp.zeros((3, 8, 128), F32)
    for part in (6, 7):
        mort[pl.ds(part, 32, stride=8), :] = jnp.zeros((32, 128), F32)
    for field in range(6):
        copies[field].wait()
        for piece, value in enumerate(split3(state[rows_of(field)])):
            pieces[piece, rows_of(field)] = value
    copies[6].wait()
    inner = (
        mm(pieces[0], select[...]) + mm(pieces[1], select[...]) + mm(pieces[2], select[...])
    )
    leaving = []
    for pair in range(3):
        even, odd = rows_of(2 * pair), rows_of(2 * pair + 1)
        fronts = [(state[even, :128], state[odd, :128])]
        backs = [(state[even, 384:], state[odd, 384:])]
        for dim in range(2):
            at = slice(128 * dim, 128 * dim + 128)
            fronts.append((inner[even, at], inner[odd, at]))
        backs += fronts[1:]
        for dim in range(3):
            front = jnp.where(low, fronts[dim][0], swap_halves(fronts[dim][1]))
            back = jnp.where(low, swap_halves(backs[dim][0]), backs[dim][1])
            table[pair, pl.ds(2 * dim, 128, stride=6), :] = front
            table[pair, pl.ds(2 * dim + 1, 128, stride=6), :] = back
        leaving += start_all([table.at[pair, 0:768]], [table_far.at[pair]], sent.at[7 + pair : 8 + pair])
    for copy in copies[7:]:
        copy.wait()

    def move(out, row, slot):
        for pair in range(3):
            out[row : row + 1, 128 * pair : 128 * pair + 128] = table[pair, pl.ds(slot, 1), :]

    for q in range(4):
        for at in range(32):
            move(picked, 32 + 32 * q + at, slot_or_spare(child[q, at]))
    for at in range(32):
        move(picked, at, slot_or_spare(owner[0, at]))
    for o, out in enumerate((s0_far, s1_far, s2_far, s3_far)):
        for at in range(32):
            move(picked, 160 + 32 * o + at, send[o, at])
        leaving += start_all([picked.at[160 + 32 * o : 192 + 32 * o]], [out], sent.at[2 + o : 3 + o])
    leaving += start_all([picked.at[0:32]], [large_far], sent.at[1:2])
    for part in range(3):
        mort[pl.ds(3 + part, 32, stride=8), :] = picked[0:32, 128 * part : 128 * part + 128]
    stacked = jnp.concatenate(
        [
            jnp.concatenate(
                [
                    picked[32 + 32 * q : 64 + 32 * q, 128 * part : 128 * part + 128]
                    for q in range(4)
                ],
                1,
            )
            for part in range(3)
        ],
        0,
    )
    back = jnp.dot(stacked, restrict[...], precision=HIGHEST, preferred_element_type=F32)
    for part in range(3):
        mort[pl.ds(part, 32, stride=8), :] = back[32 * part : 32 * part + 32]
    leaving += start_all([mort], [mort_far], sent.at[6:7])
    for copy in leaving:
        copy.wait()


def wanted_column(sources, face):
    down = lax.broadcasted_iota(jnp.int32, (128, 128), 0)
    across = lax.broadcasted_iota(jnp.int32, (128, 128), 1)
    spread = jnp.zeros((128, 128), F32)
    for part in range(6):
        hit = across + 128 * part == 6 * down + face
        spread = jnp.where(hit, sources[part : part + 1], spread)
    return jnp.sum(spread, axis=1, keepdims=True).astype(jnp.int32)


def add_owned(jumps, owner, levels, rows, sign):
    for at in range(32):
        slot = owner[0, at]
        element = jnp.where(slot < 0, 0, (slot * 10923) >> 16)
        scale = sign * (1 << levels[0, element]).astype(F32)
        row = (slot - 6 * element) * 128 + element
        target = pl.ds(jnp.where(slot < 0, 768, row), 1)
        jumps[target] = jumps[target] + scale * rows[at : at + 1]


def by_field_order(jumps, values, dim):
    low = low_half(128)
    at = slice(128 * dim, 128 * dim + 128)
    for pair in range(3):
        lanes = slice(128 * pair, 128 * pair + 128)
        front = jumps[256 * dim : 256 * dim + 128, lanes]
        back = jumps[256 * dim + 128 : 256 * dim + 256, lanes]
        values[rows_of(2 * pair), at] = jnp.where(low, front, swap_halves(back))
        values[rows_of(2 * pair + 1), at] = jnp.where(low, swap_halves(front), back)


def add_surface(values, flux, penalty, factor, surfaces, lift, out, out_far, ready, done):
    step = 32
    low = low_half(step)
    signs = jnp.where(low, -factor, factor)
    sent = []
    for pair in range(3):
        rows = slice(256 * pair, 256 * pair + 256)
        ready(pair)
        for field in (2 * pair, 2 * pair + 1):
            drag = factor * penalty[field]
            for dim in range(3):
                lanes = slice(128 * dim, 128 * dim + 128)
                rates = [flux[dim, field, other] for other in range(6)]
                for first in range(0, 128, step):
                    mixed = rates[0] * values[first : first + step, lanes]
                    for other in range(1, 6):
                        at = 128 * other + first
                        mixed = mixed + rates[other] * values[at : at + step, lanes]
                    at = 128 * field + first
                    surface = signs * mixed - drag * values[at : at + step, lanes]
                    if dim == 0:
                        out[at : at + step, 0:128] += jnp.where(low, surface, 0.0)
                        out[at : at + step, 384:512] += jnp.where(low, 0.0, surface)
                    else:
                        high = surface.astype(BF16)
                        surfaces[at : at + step, 128 * dim - 128 : 128 * dim] = high
                        rest = (surface - high.astype(F32)).astype(BF16)
                        surfaces[at : at + step, 128 * dim + 128 : 128 * dim + 256] = rest
        out[rows] += mm(surfaces[rows], lift[...])
        copy = pltpu.make_async_copy(out.at[rows], out_far.at[rows], done.at[pair])
        copy.start()
        sent.append(copy)
    return sent


def mid_kernel(
    levels_far, child_far, source_far, flux_far, penalty_far, owner_far, state_far, d0_far, d1_far,
    d2_far, table_far, large_far, both_far, lift_far, edge, out_far,
    levels, child, source, flux, penalty, owner, levels_near, state, d0, d1, d2, table, large, both,
    lift, out, pieces, grads, matrix, amount, traces, jumps, values, surfaces,
    arrivals, sent,
):
    copies = start_all(
        [levels_far, child_far, source_far], [levels, child, source], arrivals.at[0:3]
    )
    state_copies = start_all(
        [state_far.at[rows_of(f)] for f in range(6)],
        [state.at[rows_of(f)] for f in range(6)],
        arrivals.at[3:9],
    )
    copies += [None] + start_all(
        [flux_far, penalty_far, d0_far, d1_far, d2_far, owner_far, levels_far],
        [flux, penalty, d0, d1, d2, owner, levels_near],
        arrivals.at[9:16],
    )
    later = start_all(
        [table_far, large_far, both_far, lift_far], [table, large, both, lift], arrivals.at[17:21]
    )
    for copy in copies[:3]:
        copy.wait()
    level = column_of(levels[...])
    twos = (1 << level).astype(F32)
    minus = -twos
    amount[...] = jnp.broadcast_to(minus * STEP_SIZE, (128, 128))
    slots = lax.broadcasted_iota(jnp.int32, (1, 768), 1)
    element = lax.broadcasted_iota(jnp.int32, (128, 1), 0)
    child_row = jnp.concatenate([child[q : q + 1, :] for q in range(4)], 1)
    sources = source[...].astype(F32)
    for face in range(6):
        wanted = wanted_column(sources, face)
        mine = 6 * element + face
        rows = rows_of(face)
        as_child = jnp.where(mine == child_row, twos, 0.0)
        own = jnp.where(wanted >= 0, twos, 0.0) + jnp.sum(as_child, axis=1, keepdims=True)
        for other in range(6):
            at = slots[:, rows_of(other)]
            block = jnp.where(wanted == at, minus, 0.0) + jnp.where(mine == at, own, 0.0)
            matrix[rows, rows_of(other)] = block.astype(BF16)
    for field in range(6):
        state_copies[field].wait()
        rows = rows_of(field)
        value = state[rows]
        high = value.astype(BF16)
        pieces[0, rows] = high
        pieces[1, rows] = (value - high.astype(F32)).astype(BF16)
    for copy in copies[4:11] + later:
        copy.wait()

    for pair in range(3):
        for piece, value in enumerate(split3(table[pair])):
            first = 384 * piece + 128 * pair
            traces[:, first : first + 128] = value
    back = jnp.concatenate(
        [
            jnp.dot(
                large[:, 128 * part : 128 * part + 128],
                both[...],
                precision=HIGHEST,
                preferred_element_type=F32,
            )
            for part in range(3)
        ],
        1,
    )
    jumps[...] = jnp.zeros((776, 384), F32)
    add_owned(jumps, owner, levels_near, back, 1.0)

    def apply(lanes, deriv):
        high, rest = pieces[0, :, lanes], pieces[1, :, lanes]
        return mm(high, deriv[0]) + (mm(high, deriv[1]) + mm(rest, deriv[0]))

    grads[0] = apply(slice(0, 512), d0)
    for half in range(2):
        lanes = slice(256 * half, 256 * half + 256)
        grads[1, :, lanes] = apply(lanes, d1)
        grads[2, :, lanes] = apply(lanes, d2)
    def mix(first):
        scale = amount[first : first + 16]
        scale = jnp.concatenate([scale] * 4, 1)
        for field in range(6):
            total = None
            for dim in range(3):
                for other in range(6):
                    rows = slice(128 * other + first, 128 * other + first + 16)
                    term = flux[dim, field, other] * grads[dim, rows, :]
                    total = term if total is None else total + term
            out[128 * field + first : 128 * field + first + 16] = scale * total

    for dim in range(3):
        rows = slice(256 * dim, 256 * dim + 256)
        total = mm(matrix[rows], traces[...])
        for first in range(48 * dim, min(48 * dim + 48, 128), 16):
            mix(first)
        jumps[rows] += total[:, 0:384] + total[:, 384:768] + total[:, 768:1152]
        by_field_order(jumps, values, dim)
    leaving = add_surface(
        values, flux, penalty, 0.5 * STEP_SIZE * edge, surfaces, lift, out, out_far,
        lambda pair: None, sent,
    )
    for copy in leaving:
        copy.wait()


def post_kernel(
    got, a0, a1, a2, a3, project, source, child, levels_row, flux_far, penalty_far, owner_far,
    levels_far, lift_far, local_far, edge, out_far,
    flux, penalty, owner, levels, lift, out, remote, extra, jumps, values, surfaces,
    arrivals, done,
):
    thirds = [slice(256 * pair, 256 * pair + 256) for pair in range(3)]
    copies = start_all(
        [flux_far, penalty_far, owner_far, levels_far, lift_far, *(local_far.at[rows] for rows in thirds)],
        [flux, penalty, owner, levels, lift, *(out.at[rows] for rows in thirds)],
        arrivals,
    )
    minus = -(1 << column_of(levels_row[...])).astype(F32)
    element = lax.broadcasted_iota(jnp.int32, (128, 1), 0)
    arrived_slot = 768 + lax.broadcasted_iota(jnp.int32, (1, 128), 1)
    child_row = jnp.concatenate([child[q : q + 1, :] for q in range(4)], 1)
    sources = source[...].astype(F32)
    for face in range(6):
        wanted, mine = wanted_column(sources, face), 6 * element + face
        remote[rows_of(face), 0:128] = jnp.where(wanted == arrived_slot, minus, 0.0).astype(BF16)
        remote[rows_of(face), 128:256] = jnp.where(mine == child_row, minus, 0.0).astype(BF16)
    for place, rows in enumerate((a0, a1, a2, a3)):
        for piece, value in enumerate(split3(rows[...])):
            extra[32 * place : 32 * place + 32, 384 * piece : 384 * piece + 384] = value
    got_back = [got[pl.ds(part, 32, stride=8), :] for part in range(3)]
    got_large = [got[pl.ds(3 + part, 32, stride=8), :] for part in range(3)]
    onto = jnp.dot(
        jnp.concatenate(got_large, 0), project[...], precision=HIGHEST, preferred_element_type=F32
    )
    for piece, value in enumerate(split3(onto)):
        for part in range(3):
            lanes = slice(384 * piece + 128 * part, 384 * piece + 128 * part + 128)
            for q in range(4):
                extra[128 + 32 * q : 160 + 32 * q, lanes] = value[
                    32 * part : 32 * part + 32, 128 * q : 128 * q + 128
                ]
    for copy in copies[:5]:
        copy.wait()
    jumps[...] = jnp.zeros((776, 384), F32)
    add_owned(jumps, owner, levels, jnp.concatenate(got_back, 1), -1.0)
    for dim in range(3):
        rows = slice(256 * dim, 256 * dim + 256)
        total = mm(remote[rows], extra[...])
        jumps[rows] += total[:, 0:384] + total[:, 384:768] + total[:, 768:1152]
        by_field_order(jumps, values, dim)
    sent = add_surface(
        values, flux, penalty, 0.5 * STEP_SIZE * edge, surfaces, lift, out, out_far,
        lambda pair: copies[5 + pair].wait(), done,
    )
    for copy in sent:
        copy.wait()


def per_device(state, levels, face_source, face_send, mort_owner, mort_child, flux_jac, penalty):
    tables = basis_tables(P_SIZE)
    by_field = state.transpose(1, 0, 2).reshape(768, 512)
    send = face_send.reshape(4, 32)
    owner = mort_owner.reshape(1, 32)
    child = mort_child.transpose(0, 2, 1).reshape(4, 32)

    def shape(dims, kind=F32):
        return jax.ShapeDtypeStruct(dims, kind)

    def params(mib):
        return pltpu.CompilerParams(vmem_limit_bytes=mib * MIB)

    s0, s1, s2, s3, mort, table, large = pl.pallas_call(
        pre_kernel,
        out_shape=[shape((32, 384))] * 4
        + [shape((256, 128)), shape((3, 768, 128)), shape((32, 384))],
        in_specs=[HBM] * 6,
        out_specs=[HBM] * 7,
        scratch_shapes=[
            pltpu.VMEM((768, 512), F32),
            pltpu.SMEM((4, 32), jnp.int32),
            pltpu.SMEM((1, 32), jnp.int32),
            pltpu.SMEM((4, 32), jnp.int32),
            pltpu.VMEM((512, 256), BF16),
            pltpu.VMEM((512, 128), F32),
            pltpu.VMEM((3, 768, 512), BF16),
            pltpu.VMEM((3, 776, 128), F32),
            pltpu.VMEM((288, 384), F32),
            pltpu.VMEM((256, 128), F32),
            pltpu.SemaphoreType.DMA((11,)),
            pltpu.SemaphoreType.DMA((10,)),
        ],
        compiler_params=params(60),
        cost_estimate=pl.CostEstimate(flops=10**9, bytes_accessed=4 << 20, transcendentals=0),
        name="pre",
    )(by_field, send, owner, child, tables["select"], tables["restrict"])
    arrived = [
        shifted(rows, ("gx", "gy"), OFFSETS[place]) for place, rows in enumerate((s0, s1, s2, s3))
    ]
    got = lax.all_to_all(mort.reshape(32, 8, 128), "gy", split_axis=0, concat_axis=0, tiled=True)
    edge = tables["edge"]

    def mid(*refs):
        mid_kernel(*refs[:14], edge, *refs[14:])

    local = pl.pallas_call(
        mid,
        out_shape=shape((768, 512)),
        in_specs=[HBM] * 14,
        out_specs=HBM,
        scratch_shapes=[
            pltpu.VMEM((1, 128), jnp.int32),
            pltpu.VMEM((4, 32), jnp.int32),
            pltpu.VMEM((6, 128), jnp.int32),
            pltpu.SMEM((3, 6, 6), F32),
            pltpu.SMEM((6,), F32),
            pltpu.SMEM((1, 32), jnp.int32),
            pltpu.SMEM((1, 128), jnp.int32),
            pltpu.VMEM((768, 512), F32),
            pltpu.VMEM((2, 512, 512), BF16),
            pltpu.VMEM((2, 256, 256), BF16),
            pltpu.VMEM((2, 256, 256), BF16),
            pltpu.VMEM((3, 768, 128), F32),
            pltpu.VMEM((32, 384), F32),
            pltpu.VMEM((128, 128), F32),
            pltpu.VMEM((512, 512), BF16),
            pltpu.VMEM((768, 512), F32),
            pltpu.VMEM((2, 768, 512), BF16),
            pltpu.VMEM((3, 768, 512), F32),
            pltpu.VMEM((768, 768), BF16),
            pltpu.VMEM((128, 128), F32),
            pltpu.VMEM((768, 1152), BF16),
            pltpu.VMEM((776, 384), F32),
            pltpu.VMEM((768, 384), F32),
            pltpu.VMEM((768, 512), BF16),
            pltpu.SemaphoreType.DMA((21,)),
            pltpu.SemaphoreType.DMA((3,)),
        ],
        compiler_params=params(60),
        cost_estimate=pl.CostEstimate(flops=8 * 10**9, bytes_accessed=8 << 20, transcendentals=0),
        name="mid",
    )(
        levels.reshape(1, 128),
        child,
        face_source.reshape(6, 128),
        flux_jac,
        penalty,
        owner,
        by_field,
        tables["deriv_0"],
        tables["deriv_1"],
        tables["deriv_2"],
        table,
        large,
        tables["both"],
        tables["lift"],
    )

    def post(*refs):
        post_kernel(*refs[:15], edge, *refs[15:])

    result = pl.pallas_call(
        post,
        out_shape=shape((768, 512)),
        in_specs=[VMEM] * 9 + [HBM] * 6,
        out_specs=HBM,
        input_output_aliases={14: 0},
        scratch_shapes=[
            pltpu.SMEM((3, 6, 6), F32),
            pltpu.SMEM((6,), F32),
            pltpu.SMEM((1, 32), jnp.int32),
            pltpu.SMEM((1, 128), jnp.int32),
            pltpu.VMEM((512, 512), BF16),
            pltpu.VMEM((768, 512), F32),
            pltpu.VMEM((768, 256), BF16),
            pltpu.VMEM((256, 1152), BF16),
            pltpu.VMEM((776, 384), F32),
            pltpu.VMEM((768, 384), F32),
            pltpu.VMEM((768, 512), BF16),
            pltpu.SemaphoreType.DMA((8,)),
            pltpu.SemaphoreType.DMA((3,)),
        ],
        compiler_params=params(32),
        cost_estimate=pl.CostEstimate(flops=2 * 10**9, bytes_accessed=4 << 20, transcendentals=0),
        name="post",
    )(
        got.reshape(256, 128),
        *arrived,
        tables["project"],
        face_source.reshape(6, 128),
        child,
        levels.reshape(1, 128),
        flux_jac,
        penalty,
        owner,
        levels.reshape(1, 128),
        tables["lift"],
        local,
    )
    return result.reshape(6, 128, 512).transpose(1, 0, 2)


def solution(mesh):
    in_specs = (
        P(("gx", "gy"), None, None),
        P(("gx", "gy")),
        P(("gx", "gy")),
        P(("gx", "gy"), None, None),
        P(("gx", "gy"), None, None),
        P(("gx", "gy"), None, None),
        P(),
        P(),
    )
    out_specs = P(("gx", "gy"), None, None)
    return jax.shard_map(
        per_device, mesh=mesh, in_specs=in_specs, out_specs=out_specs, check_vma=False
    )
```

```python
import jax
import jax.numpy as jnp
import ml_dtypes
import numpy as np
from jax import lax
from jax.experimental import pallas as pl
from jax.experimental.pallas import tpu as pltpu
from jax.sharding import PartitionSpec as P

P_SIZE = 7
OFFSETS = (-2, -1, 1, 2)
STEP_SIZE = 0.01

F32 = jnp.float32
BF16 = jnp.bfloat16
HIGHEST = lax.Precision.HIGHEST
VMEM = pl.BlockSpec(memory_space=pltpu.VMEM)
HBM = pl.BlockSpec(memory_space=pltpu.HBM)
MIB = 1 << 20


def shifted(value, axis, steps):
    count = lax.axis_size(axis)
    pairs = [(source, (source + steps) % count) for source in range(count)]
    return lax.ppermute(value, axis, pairs)


def pieces_of(table):
    rest = np.asarray(table, np.float32)
    out = []
    for _ in range(2):
        piece = rest.astype(ml_dtypes.bfloat16)
        out.append(piece)
        rest = rest - piece.astype(np.float32)
    return np.stack(out)


def basis_tables(order):
    per_dim = order + 1
    eye_small = np.eye(per_dim)
    points = -np.cos(np.pi * np.arange(per_dim) / order)
    differences = points[:, None] - points[None, :] + eye_small
    barycentric = 1.0 / np.prod(differences, axis=1)
    derivative = barycentric[None, :] / barycentric[:, None] / differences
    derivative = np.where(eye_small > 0, 0.0, derivative)
    derivative = derivative - eye_small * derivative.sum(axis=1)[:, None]
    angles = np.pi * np.arange(per_dim) / order
    weights = np.ones(per_dim)
    for wave in range(1, order // 2 + 1):
        factor = 1.0 if 2 * wave == order else 2.0
        weights = weights - factor * np.cos(2.0 * wave * angles) / (4.0 * wave * wave - 1.0)
    edge_factor = np.where((np.arange(per_dim) == 0) | (np.arange(per_dim) == order), 1.0, 2.0)
    weights = edge_factor * weights / order

    def lagrange(targets):
        values_at = np.ones((per_dim, per_dim))
        for column in range(per_dim):
            for other in range(per_dim):
                if other != column:
                    values_at[:, column] *= (targets - points[other]) / (
                        points[column] - points[other]
                    )
        return values_at

    halves = [lagrange((points - 1.0) / 2.0), lagrange((points + 1.0) / 2.0)]
    identity = np.eye(per_dim)
    node_index = np.arange(per_dim**3).reshape(per_dim, per_dim, per_dim)
    fnodes = per_dim * per_dim
    select = np.zeros((per_dim**3, 4 * fnodes), np.float32)
    for face in range(2, 6):
        picker = [slice(None), slice(None), slice(None)]
        picker[face // 2] = 0 if face % 2 == 0 else order
        on_face = node_index[tuple(picker)].reshape(-1)
        select[on_face, (face - 2) * fnodes + np.arange(fnodes)] = 1.0
    face_weight = np.kron(weights, weights)
    proj = [np.kron(halves[quad // 2], halves[quad % 2]) for quad in range(4)]
    restrict = [
        0.25 * (proj[quad].T * face_weight[None, :]) / face_weight[:, None] for quad in range(4)
    ]
    two = np.eye(2)
    both = sum(restrict[quad] @ proj[quad] for quad in range(4))
    quarter = np.eye(4)
    return {
        "select": select.astype(ml_dtypes.bfloat16),
        "lift": np.concatenate([select.T, select.T], 0).astype(ml_dtypes.bfloat16),
        "restrict": np.concatenate([np.kron(two, r.T) for r in restrict], 0).astype(np.float32),
        "project": np.concatenate([np.kron(two, p.T) for p in proj], 1).astype(np.float32),
        "both": np.kron(two, both.T).astype(np.float32),
        "deriv_0": pieces_of(np.kron(derivative, np.eye(fnodes)).T),
        "deriv_1": pieces_of(np.kron(quarter, np.kron(derivative, identity)).T),
        "deriv_2": pieces_of(np.kron(quarter, np.kron(identity, derivative)).T),
        "edge": float(1.0 / weights[0]),
    }


def split3(value):
    high = value.astype(BF16)
    rest = value - high.astype(F32)
    middle = rest.astype(BF16)
    low = (rest - middle.astype(F32)).astype(BF16)
    return high, middle, low


def mm(a, b):
    return jnp.dot(a, b, preferred_element_type=F32)


def low_half(rows):
    return lax.broadcasted_iota(jnp.int32, (rows, 128), 1) < 64


def swap_halves(value):
    return pltpu.roll(value, 64, 1)


def column_of(row):
    count = row.shape[1]
    spread = jnp.broadcast_to(row.astype(F32), (count, count))
    down = lax.broadcasted_iota(jnp.int32, (count, count), 0)
    across = lax.broadcasted_iota(jnp.int32, (count, count), 1)
    return jnp.sum(jnp.where(down == across, spread, 0.0), axis=1, keepdims=True).astype(jnp.int32)


def start_all(sources, targets, arrivals):
    copies = [
        pltpu.make_async_copy(source, target, arrivals.at[at])
        for at, (source, target) in enumerate(zip(sources, targets, strict=True))
    ]
    for copy in copies:
        copy.start()
    return copies


def rows_of(field):
    return slice(128 * field, 128 * field + 128)


def slot_or_spare(slot):
    return jnp.where(slot < 0, 768, slot)


def pre_kernel(
    state_far, send_far, owner_far, child_far, select_far, restrict_far,
    s0_far, s1_far, s2_far, s3_far, mort_far, table_far, large_far,
    state, send, owner, child, select, restrict, pieces, table, picked, mort, arrivals, sent,
):
    copies = start_all(
        [*(state_far.at[rows_of(f)] for f in range(6)), select_far, send_far, owner_far, child_far, restrict_far],
        [*(state.at[rows_of(f)] for f in range(6)), select, send, owner, child, restrict],
        arrivals,
    )
    low = low_half(128)
    table[:, 768:776] = jnp.zeros((3, 8, 128), F32)
    for part in (6, 7):
        mort[pl.ds(part, 32, stride=8), :] = jnp.zeros((32, 128), F32)
    for field in range(6):
        copies[field].wait()
        for piece, value in enumerate(split3(state[rows_of(field)])):
            pieces[piece, rows_of(field)] = value
    copies[6].wait()
    inner = (
        mm(pieces[0], select[...]) + mm(pieces[1], select[...]) + mm(pieces[2], select[...])
    )
    leaving = []
    for pair in range(3):
        even, odd = rows_of(2 * pair), rows_of(2 * pair + 1)
        fronts = [(state[even, :128], state[odd, :128])]
        backs = [(state[even, 384:], state[odd, 384:])]
        for dim in range(2):
            at = slice(128 * dim, 128 * dim + 128)
            fronts.append((inner[even, at], inner[odd, at]))
        backs += fronts[1:]
        for dim in range(3):
            front = jnp.where(low, fronts[dim][0], swap_halves(fronts[dim][1]))
            back = jnp.where(low, swap_halves(backs[dim][0]), backs[dim][1])
            table[pair, pl.ds(2 * dim, 128, stride=6), :] = front
            table[pair, pl.ds(2 * dim + 1, 128, stride=6), :] = back
        leaving += start_all([table.at[pair, 0:768]], [table_far.at[pair]], sent.at[7 + pair : 8 + pair])
    for copy in copies[7:]:
        copy.wait()

    def move(out, row, slot):
        for pair in range(3):
            out[row : row + 1, 128 * pair : 128 * pair + 128] = table[pair, pl.ds(slot, 1), :]

    for q in range(4):
        for at in range(32):
            move(picked, 32 + 32 * q + at, slot_or_spare(child[q, at]))
    for at in range(32):
        move(picked, at, slot_or_spare(owner[0, at]))
    for o, out in enumerate((s0_far, s1_far, s2_far, s3_far)):
        for at in range(32):
            move(picked, 160 + 32 * o + at, send[o, at])
        leaving += start_all([picked.at[160 + 32 * o : 192 + 32 * o]], [out], sent.at[2 + o : 3 + o])
    leaving += start_all([picked.at[0:32]], [large_far], sent.at[1:2])
    for part in range(3):
        mort[pl.ds(3 + part, 32, stride=8), :] = picked[0:32, 128 * part : 128 * part + 128]
    stacked = jnp.concatenate(
        [
            jnp.concatenate(
                [
                    picked[32 + 32 * q : 64 + 32 * q, 128 * part : 128 * part + 128]
                    for q in range(4)
                ],
                1,
            )
            for part in range(3)
        ],
        0,
    )
    back = jnp.dot(stacked, restrict[...], precision=HIGHEST, preferred_element_type=F32)
    for part in range(3):
        mort[pl.ds(part, 32, stride=8), :] = back[32 * part : 32 * part + 32]
    leaving += start_all([mort], [mort_far], sent.at[6:7])
    for copy in leaving:
        copy.wait()


def wanted_column(sources, face):
    down = lax.broadcasted_iota(jnp.int32, (128, 128), 0)
    across = lax.broadcasted_iota(jnp.int32, (128, 128), 1)
    spread = jnp.zeros((128, 128), F32)
    for part in range(6):
        hit = across + 128 * part == 6 * down + face
        spread = jnp.where(hit, sources[part : part + 1], spread)
    return jnp.sum(spread, axis=1, keepdims=True).astype(jnp.int32)


def add_owned(jumps, owner, levels, rows, sign):
    for at in range(32):
        slot = owner[0, at]
        element = jnp.where(slot < 0, 0, (slot * 10923) >> 16)
        scale = sign * (1 << levels[0, element]).astype(F32)
        row = (slot - 6 * element) * 128 + element
        target = pl.ds(jnp.where(slot < 0, 768, row), 1)
        jumps[target] = jumps[target] + scale * rows[at : at + 1]


def by_field_order(jumps, values, dim):
    low = low_half(128)
    at = slice(128 * dim, 128 * dim + 128)
    for pair in range(3):
        lanes = slice(128 * pair, 128 * pair + 128)
        front = jumps[256 * dim : 256 * dim + 128, lanes]
        back = jumps[256 * dim + 128 : 256 * dim + 256, lanes]
        values[rows_of(2 * pair), at] = jnp.where(low, front, swap_halves(back))
        values[rows_of(2 * pair + 1), at] = jnp.where(low, swap_halves(front), back)


def add_surface(values, flux, penalty, factor, surfaces, lift, out, out_far, ready, done):
    step = 32
    low = low_half(step)
    signs = jnp.where(low, -factor, factor)
    sent = []
    for pair in range(3):
        rows = slice(256 * pair, 256 * pair + 256)
        ready(pair)
        for field in (2 * pair, 2 * pair + 1):
            drag = factor * penalty[field]
            for dim in range(3):
                lanes = slice(128 * dim, 128 * dim + 128)
                rates = [flux[dim, field, other] for other in range(6)]
                for first in range(0, 128, step):
                    mixed = rates[0] * values[first : first + step, lanes]
                    for other in range(1, 6):
                        at = 128 * other + first
                        mixed = mixed + rates[other] * values[at : at + step, lanes]
                    at = 128 * field + first
                    surface = signs * mixed - drag * values[at : at + step, lanes]
                    if dim == 0:
                        out[at : at + step, 0:128] += jnp.where(low, surface, 0.0)
                        out[at : at + step, 384:512] += jnp.where(low, 0.0, surface)
                    else:
                        high = surface.astype(BF16)
                        surfaces[at : at + step, 128 * dim - 128 : 128 * dim] = high
                        rest = (surface - high.astype(F32)).astype(BF16)
                        surfaces[at : at + step, 128 * dim + 128 : 128 * dim + 256] = rest
        out[rows] += mm(surfaces[rows], lift[...])
        copy = pltpu.make_async_copy(out.at[rows], out_far.at[rows], done.at[pair])
        copy.start()
        sent.append(copy)
    return sent


def mid_kernel(
    levels_far, child_far, source_far, flux_far, penalty_far, owner_far, state_far, d0_far, d1_far,
    d2_far, table_far, large_far, both_far, lift_far, edge, out_far,
    levels, child, source, flux, penalty, owner, levels_near, state, d0, d1, d2, table, large, both,
    lift, out, pieces, grads, matrix, amount, traces, jumps, values, surfaces,
    arrivals, sent,
):
    copies = start_all(
        [levels_far, child_far, source_far], [levels, child, source], arrivals.at[0:3]
    )
    state_copies = start_all(
        [state_far.at[rows_of(f)] for f in range(6)],
        [state.at[rows_of(f)] for f in range(6)],
        arrivals.at[3:9],
    )
    copies += [None] + start_all(
        [flux_far, penalty_far, d0_far, d1_far, d2_far, owner_far, levels_far],
        [flux, penalty, d0, d1, d2, owner, levels_near],
        arrivals.at[9:16],
    )
    later = start_all(
        [table_far, large_far, both_far, lift_far], [table, large, both, lift], arrivals.at[17:21]
    )
    for copy in copies[:3]:
        copy.wait()
    level = column_of(levels[...])
    twos = (1 << level).astype(F32)
    minus = -twos
    amount[...] = jnp.broadcast_to(minus * STEP_SIZE, (128, 128))
    slots = lax.broadcasted_iota(jnp.int32, (1, 768), 1)
    element = lax.broadcasted_iota(jnp.int32, (128, 1), 0)
    child_row = jnp.concatenate([child[q : q + 1, :] for q in range(4)], 1)
    sources = source[...].astype(F32)
    for face in range(6):
        wanted = wanted_column(sources, face)
        mine = 6 * element + face
        rows = rows_of(face)
        as_child = jnp.where(mine == child_row, twos, 0.0)
        own = jnp.where(wanted >= 0, twos, 0.0) + jnp.sum(as_child, axis=1, keepdims=True)
        for other in range(6):
            at = slots[:, rows_of(other)]
            block = jnp.where(wanted == at, minus, 0.0) + jnp.where(mine == at, own, 0.0)
            matrix[rows, rows_of(other)] = block.astype(BF16)
    for field in range(6):
        state_copies[field].wait()
        rows = rows_of(field)
        value = state[rows]
        high = value.astype(BF16)
        pieces[0, rows] = high
        pieces[1, rows] = (value - high.astype(F32)).astype(BF16)
    for copy in copies[4:11] + later:
        copy.wait()

    for pair in range(3):
        for piece, value in enumerate(split3(table[pair])):
            first = 384 * piece + 128 * pair
            traces[:, first : first + 128] = value
    back = jnp.concatenate(
        [
            jnp.dot(
                large[:, 128 * part : 128 * part + 128],
                both[...],
                precision=HIGHEST,
                preferred_element_type=F32,
            )
            for part in range(3)
        ],
        1,
    )
    jumps[...] = jnp.zeros((776, 384), F32)
    add_owned(jumps, owner, levels_near, back, 1.0)

    def apply(lanes, deriv):
        high, rest = pieces[0, :, lanes], pieces[1, :, lanes]
        return mm(high, deriv[0]) + (mm(high, deriv[1]) + mm(rest, deriv[0]))

    grads[0] = apply(slice(0, 512), d0)
    for half in range(2):
        lanes = slice(256 * half, 256 * half + 256)
        grads[1, :, lanes] = apply(lanes, d1)
        grads[2, :, lanes] = apply(lanes, d2)
    def mix(first):
        scale = amount[first : first + 16]
        scale = jnp.concatenate([scale] * 4, 1)
        for field in range(6):
            total = None
            for dim in range(3):
                for other in range(6):
                    rows = slice(128 * other + first, 128 * other + first + 16)
                    term = flux[dim, field, other] * grads[dim, rows, :]
                    total = term if total is None else total + term
            out[128 * field + first : 128 * field + first + 16] = scale * total

    for dim in range(3):
        rows = slice(256 * dim, 256 * dim + 256)
        total = mm(matrix[rows], traces[...])
        for first in ((0, 16), (32, 48, 64), (80, 96, 112))[dim]:
            mix(first)
        jumps[rows] += total[:, 0:384] + total[:, 384:768] + total[:, 768:1152]
        by_field_order(jumps, values, dim)
    leaving = add_surface(
        values, flux, penalty, 0.5 * STEP_SIZE * edge, surfaces, lift, out, out_far,
        lambda pair: None, sent,
    )
    for copy in leaving:
        copy.wait()


def post_kernel(
    got, a0, a1, a2, a3, project, source, child, levels_row, flux_far, penalty_far, owner_far,
    levels_far, lift_far, local_far, edge, out_far,
    flux, penalty, owner, levels, lift, out, remote, extra, jumps, values, surfaces,
    arrivals, done,
):
    thirds = [slice(256 * pair, 256 * pair + 256) for pair in range(3)]
    copies = start_all(
        [flux_far, penalty_far, owner_far, levels_far, lift_far, *(local_far.at[rows] for rows in thirds)],
        [flux, penalty, owner, levels, lift, *(out.at[rows] for rows in thirds)],
        arrivals,
    )
    for place, rows in enumerate((a0, a1, a2, a3)):
        for piece, value in enumerate(split3(rows[...])):
            extra[32 * place : 32 * place + 32, 384 * piece : 384 * piece + 384] = value
    got_back = [got[pl.ds(part, 32, stride=8), :] for part in range(3)]
    got_large = [got[pl.ds(3 + part, 32, stride=8), :] for part in range(3)]
    onto = jnp.dot(
        jnp.concatenate(got_large, 0), project[...], precision=HIGHEST, preferred_element_type=F32
    )
    for piece, value in enumerate(split3(onto)):
        for part in range(3):
            lanes = slice(384 * piece + 128 * part, 384 * piece + 128 * part + 128)
            for q in range(4):
                extra[128 + 32 * q : 160 + 32 * q, lanes] = value[
                    32 * part : 32 * part + 32, 128 * q : 128 * q + 128
                ]
    minus = -(1 << column_of(levels_row[...])).astype(F32)
    element = lax.broadcasted_iota(jnp.int32, (128, 1), 0)
    arrived_slot = 768 + lax.broadcasted_iota(jnp.int32, (1, 128), 1)
    child_row = jnp.concatenate([child[q : q + 1, :] for q in range(4)], 1)
    sources = source[...].astype(F32)
    for face in range(6):
        wanted, mine = wanted_column(sources, face), 6 * element + face
        remote[rows_of(face), 0:128] = jnp.where(wanted == arrived_slot, minus, 0.0).astype(BF16)
        remote[rows_of(face), 128:256] = jnp.where(mine == child_row, minus, 0.0).astype(BF16)
    for copy in copies[:5]:
        copy.wait()
    jumps[...] = jnp.zeros((776, 384), F32)
    add_owned(jumps, owner, levels, jnp.concatenate(got_back, 1), -1.0)
    for dim in range(3):
        rows = slice(256 * dim, 256 * dim + 256)
        total = mm(remote[rows], extra[...])
        jumps[rows] += total[:, 0:384] + total[:, 384:768] + total[:, 768:1152]
        by_field_order(jumps, values, dim)
    sent = add_surface(
        values, flux, penalty, 0.5 * STEP_SIZE * edge, surfaces, lift, out, out_far,
        lambda pair: copies[5 + pair].wait(), done,
    )
    for copy in sent:
        copy.wait()


def per_device(state, levels, face_source, face_send, mort_owner, mort_child, flux_jac, penalty):
    tables = basis_tables(P_SIZE)
    by_field = state.transpose(1, 0, 2).reshape(768, 512)
    send = face_send.reshape(4, 32)
    owner = mort_owner.reshape(1, 32)
    child = mort_child.transpose(0, 2, 1).reshape(4, 32)

    def shape(dims, kind=F32):
        return jax.ShapeDtypeStruct(dims, kind)

    def params(mib):
        return pltpu.CompilerParams(vmem_limit_bytes=mib * MIB)

    s0, s1, s2, s3, mort, table, large = pl.pallas_call(
        pre_kernel,
        out_shape=[shape((32, 384))] * 4
        + [shape((256, 128)), shape((3, 768, 128)), shape((32, 384))],
        in_specs=[HBM] * 6,
        out_specs=[HBM] * 7,
        scratch_shapes=[
            pltpu.VMEM((768, 512), F32),
            pltpu.SMEM((4, 32), jnp.int32),
            pltpu.SMEM((1, 32), jnp.int32),
            pltpu.SMEM((4, 32), jnp.int32),
            pltpu.VMEM((512, 256), BF16),
            pltpu.VMEM((512, 128), F32),
            pltpu.VMEM((3, 768, 512), BF16),
            pltpu.VMEM((3, 776, 128), F32),
            pltpu.VMEM((288, 384), F32),
            pltpu.VMEM((256, 128), F32),
            pltpu.SemaphoreType.DMA((11,)),
            pltpu.SemaphoreType.DMA((10,)),
        ],
        compiler_params=params(60),
        cost_estimate=pl.CostEstimate(flops=10**9, bytes_accessed=4 << 20, transcendentals=0),
        name="pre",
    )(by_field, send, owner, child, tables["select"], tables["restrict"])
    arrived = [
        shifted(rows, ("gx", "gy"), OFFSETS[place]) for place, rows in enumerate((s0, s1, s2, s3))
    ]
    got = lax.all_to_all(mort.reshape(32, 8, 128), "gy", split_axis=0, concat_axis=0, tiled=True)
    edge = tables["edge"]

    def mid(*refs):
        mid_kernel(*refs[:14], edge, *refs[14:])

    local = pl.pallas_call(
        mid,
        out_shape=shape((768, 512)),
        in_specs=[HBM] * 14,
        out_specs=HBM,
        scratch_shapes=[
            pltpu.VMEM((1, 128), jnp.int32),
            pltpu.VMEM((4, 32), jnp.int32),
            pltpu.VMEM((6, 128), jnp.int32),
            pltpu.SMEM((3, 6, 6), F32),
            pltpu.SMEM((6,), F32),
            pltpu.SMEM((1, 32), jnp.int32),
            pltpu.SMEM((1, 128), jnp.int32),
            pltpu.VMEM((768, 512), F32),
            pltpu.VMEM((2, 512, 512), BF16),
            pltpu.VMEM((2, 256, 256), BF16),
            pltpu.VMEM((2, 256, 256), BF16),
            pltpu.VMEM((3, 768, 128), F32),
            pltpu.VMEM((32, 384), F32),
            pltpu.VMEM((128, 128), F32),
            pltpu.VMEM((512, 512), BF16),
            pltpu.VMEM((768, 512), F32),
            pltpu.VMEM((2, 768, 512), BF16),
            pltpu.VMEM((3, 768, 512), F32),
            pltpu.VMEM((768, 768), BF16),
            pltpu.VMEM((128, 128), F32),
            pltpu.VMEM((768, 1152), BF16),
            pltpu.VMEM((776, 384), F32),
            pltpu.VMEM((768, 384), F32),
            pltpu.VMEM((768, 512), BF16),
            pltpu.SemaphoreType.DMA((21,)),
            pltpu.SemaphoreType.DMA((3,)),
        ],
        compiler_params=params(60),
        cost_estimate=pl.CostEstimate(flops=8 * 10**9, bytes_accessed=8 << 20, transcendentals=0),
        name="mid",
    )(
        levels.reshape(1, 128),
        child,
        face_source.reshape(6, 128),
        flux_jac,
        penalty,
        owner,
        by_field,
        tables["deriv_0"],
        tables["deriv_1"],
        tables["deriv_2"],
        table,
        large,
        tables["both"],
        tables["lift"],
    )

    def post(*refs):
        post_kernel(*refs[:15], edge, *refs[15:])

    result = pl.pallas_call(
        post,
        out_shape=shape((768, 512)),
        in_specs=[VMEM] * 9 + [HBM] * 6,
        out_specs=HBM,
        input_output_aliases={14: 0},
        scratch_shapes=[
            pltpu.SMEM((3, 6, 6), F32),
            pltpu.SMEM((6,), F32),
            pltpu.SMEM((1, 32), jnp.int32),
            pltpu.SMEM((1, 128), jnp.int32),
            pltpu.VMEM((512, 512), BF16),
            pltpu.VMEM((768, 512), F32),
            pltpu.VMEM((768, 256), BF16),
            pltpu.VMEM((256, 1152), BF16),
            pltpu.VMEM((776, 384), F32),
            pltpu.VMEM((768, 384), F32),
            pltpu.VMEM((768, 512), BF16),
            pltpu.SemaphoreType.DMA((8,)),
            pltpu.SemaphoreType.DMA((3,)),
        ],
        compiler_params=params(32),
        cost_estimate=pl.CostEstimate(flops=2 * 10**9, bytes_accessed=4 << 20, transcendentals=0),
        name="post",
    )(
        got.reshape(256, 128),
        *arrived,
        tables["project"],
        face_source.reshape(6, 128),
        child,
        levels.reshape(1, 128),
        flux_jac,
        penalty,
        owner,
        levels.reshape(1, 128),
        tables["lift"],
        local,
    )
    return result.reshape(6, 128, 512).transpose(1, 0, 2)


def solution(mesh):
    in_specs = (
        P(("gx", "gy"), None, None),
        P(("gx", "gy")),
        P(("gx", "gy")),
        P(("gx", "gy"), None, None),
        P(("gx", "gy"), None, None),
        P(("gx", "gy"), None, None),
        P(),
        P(),
    )
    out_specs = P(("gx", "gy"), None, None)
    return jax.shard_map(
        per_device, mesh=mesh, in_specs=in_specs, out_specs=out_specs, check_vma=False
    )
```
